32 devices in a mesh: shard: 8 (over y, x, core), ctx: 4 (over z).
Axes of the slice: x: 2, y: 2, z: 4, core: 2. Of those that a mesh axis runs over, the one named last changes fastest.
Arguments:
- tokens: bfloat16 [8, 1536, 768], P('shard', 'ctx'), may hold values from -6 to 6
- cotangent: bfloat16 [8, 1536, 768], P('shard', 'ctx'), may hold values from -6 to 6
- doc_lengths: int32 [8, 4], P('shard'), may hold values from 0 to 1536, as said below
- w_qkv: bfloat16 [768, 2304], P('shard'), may hold values from -0.21875 to 0.21875
- w_out: bfloat16 [768, 768], P('shard'), may hold values from -6 to 6
- w_in: bfloat16 [768, 3072], P('shard'), may hold values from -0.21875 to 0.21875
- w_down: bfloat16 [3072, 768], P('shard'), may hold values from -0.109375 to 0.109375
- bias_query: bfloat16 [768], P('shard'), may hold values from -1.5 to 1.5
- bias_value: bfloat16 [768], P('shard'), may hold values from -0.3125 to 0.3125
- bias_out: bfloat16 [768], P('shard'), may hold values from -1.5 to 1.5
- gain_attn: bfloat16 [768], P('shard'), may hold values from 0.5 to 1.5
- shift_attn: bfloat16 [768], P('shard'), may hold values from -3 to 3
- bias_in: bfloat16 [3072], P('shard'), may hold values from -1.5 to 1.5
- bias_down: bfloat16 [768], P('shard'), may hold values from -1.5 to 1.5
- gain_ffn: bfloat16 [768], P('shard'), may hold values from 0.5 to 1.5
- shift_ffn: bfloat16 [768], P('shard'), may hold values from -3 to 3
Outputs:
- layer_out: bfloat16 [8, 1536, 768], P('shard', 'ctx')
- grad_tokens: float32 [8, 1536, 768], P('shard', 'ctx')
- grad_w_qkv: float32 [768, 2304], P('shard')
- grad_w_out: float32 [768, 768], P('shard')
- grad_w_in: float32 [768, 3072], P('shard')
- grad_w_down: float32 [3072, 768], P('shard')
- grad_bias_query: float32 [768], P('shard')
- grad_bias_value: float32 [768], P('shard')
- grad_bias_out: float32 [768], P('shard')
- grad_gain_attn: float32 [768], P('shard')
- grad_shift_attn: float32 [768], P('shard')
- grad_bias_in: float32 [3072], P('shard')
- grad_bias_down: float32 [768], P('shard')
- grad_gain_ffn: float32 [768], P('shard')
- grad_shift_ffn: float32 [768], P('shard')
The draws below stay inside these ranges and needn't reach their ends.
Inputs may be any that keep to these rules, and one draw needn't show every extreme that they name: `doc_lengths`: each row holds a sequence's document lengths in order, summing to 1536: either 2 to 4 nonzero lengths of at least 192 tokens each followed by zeros, or one document of 1536 tokens followed by zeros. In every draw at least one sequence is a single document.
All inputs are finite; a program needn't handle non-finite values.
Results may differ from the reference program's by a relative error of at most 0.02.
Values may be sent and summed in bfloat16 or wider, within the bound.
A program may use at most 128 MiB of HBM per device.

```python
import jax
import jax.numpy as jnp
from jax import lax

D = 768
HEADS = 12
HEAD = 64
FF = 3072
DOCS = 4
SEQ_LEN = 1536
SEQS = 8


def draw_doc_lengths(key, part):
    key = jax.random.fold_in(key, 11)
    key_count, key_cuts, key_pick = jax.random.split(key, 3)
    least = SEQ_LEN // 8
    count = jax.random.randint(key_count, (SEQS, 1), 2, DOCS + 1, dtype=jnp.int32)
    room = SEQ_LEN - count * least
    cuts = jax.random.randint(key_cuts, (SEQS, DOCS - 1), 0, room + 1, dtype=jnp.int32)
    slots = jnp.arange(DOCS - 1, dtype=jnp.int32)[None, :]
    cuts = jnp.where(slots < count - 1, cuts, room)
    cuts = jnp.sort(cuts, axis=1)
    zeros = jnp.zeros((SEQS, 1), jnp.int32)
    edges = jnp.concatenate([zeros, cuts, room], axis=1)
    gaps = edges[:, 1:] - edges[:, :-1]
    places = jnp.arange(DOCS, dtype=jnp.int32)[None, :]
    lengths = gaps + jnp.where(places < count, least, 0)
    picked = jax.random.randint(key_pick, (), 0, SEQS, dtype=jnp.int32)
    chosen = (jnp.arange(SEQS, dtype=jnp.int32) == picked)[:, None]
    single = jnp.where(places == 0, SEQ_LEN, 0).astype(jnp.int32)
    return jnp.where(chosen, single, lengths).astype(jnp.int32)


def level_of(key, shape, cuts, low, high):
    loudness, own = 1.0, jax.random.fold_in(key, 6)
    for dim, shards_of in cuts:
        heights = jnp.exp(jax.random.uniform(jax.random.fold_in(own, dim), (shards_of,), jnp.float32, low / len(cuts), high / len(cuts)))
        loudness = loudness * jnp.repeat(heights, shape[dim] // shards_of).reshape([-1 if axis == dim else 1 for axis in range(len(shape))])
    return loudness


def scatter_about(own_key, extent, deviation, limit, cuts=(), held_as=jnp.bfloat16):
    entries = deviation * jax.random.normal(own_key, extent, jnp.float32)
    if cuts:
        entries = entries * level_of(own_key, extent, cuts, -0.22, 0.18)
    return jnp.clip(entries, -limit, limit).astype(held_as)


def setup_inputs(seed: int = 0) -> dict:
    keys = jax.random.split(jax.random.key(seed), 17)
    return {
        "tokens": scatter_about(keys[0], (SEQS, SEQ_LEN, D), 1.0, 6.0, ((0, 8), (1, 4))),
        "cotangent": scatter_about(keys[1], (SEQS, SEQ_LEN, D), 1.0, 6.0, ((0, 8), (1, 4))),
        "doc_lengths": draw_doc_lengths(jax.random.fold_in(keys[16], 71), 0),
        "w_qkv": scatter_about(keys[3], (D, 3 * D), D ** -0.5, 0.21875, ((0, 8),)),
        "w_out": scatter_about(keys[4], (D, D), ((SEQ_LEN // 8) ** 0.5 * D ** -0.5), 6.0, ((0, 8),)),
        "w_in": scatter_about(keys[5], (D, FF), D ** -0.5, 0.21875, ((0, 8),)),
        "w_down": scatter_about(keys[6], (FF, D), FF ** -0.5, 0.109375, ((0, 8),)),
        "bias_query": scatter_about(keys[7], (D,), 0.1, 1.5, ((0, 8),)),
        "bias_value": scatter_about(keys[8], (D,), 0.02, 0.3125, ((0, 8),)),
        "bias_out": scatter_about(keys[9], (D,), 0.1, 1.5, ((0, 8),)),
        "gain_attn": jnp.clip(1.0 + 0.1 * jax.random.normal(keys[10], (D,), jnp.float32), 0.5, 1.5).astype(jnp.bfloat16),
        "shift_attn": scatter_about(keys[11], (D,), 0.2, 3.0, ((0, 8),)),
        "bias_in": scatter_about(keys[12], (FF,), 0.1, 1.5, ((0, 8),)),
        "bias_down": scatter_about(keys[13], (D,), 0.1, 1.5, ((0, 8),)),
        "gain_ffn": jnp.clip(1.0 + 0.1 * jax.random.normal(keys[14], (D,), jnp.float32), 0.5, 1.5).astype(jnp.bfloat16),
        "shift_ffn": scatter_about(keys[15], (D,), 0.2, 3.0, ((0, 8),)),
    }


@jax.custom_vjp
def low(v):
    return lax.optimization_barrier(v.astype(jnp.bfloat16)).astype(jnp.float32)

@jax.custom_vjp
def low_back(v):
    return v

def low_keep(v):
    return (low(v), None)

def low_pass(kept, grad):
    return (grad,)

def back_keep(v):
    return (v, None)

def back_low(kept, grad):
    return (low(grad),)
low.defvjp(low_keep, low_pass)
low_back.defvjp(back_keep, back_low)
epsilon = 1e-12
precise = lax.Precision.HIGHEST

def layer_norm(values, gain, shift):
    center = values - lax.optimization_barrier(jnp.mean(values, axis=-1, keepdims=True))
    spread = lax.optimization_barrier(jnp.mean(center * center, axis=-1, keepdims=True))
    return center * lax.rsqrt(spread + epsilon) * gain + shift

def segment_ids(counts, length):
    places = jnp.arange(length, dtype=jnp.int32)
    first_end = counts[0]
    second_end = first_end + counts[1]
    third_end = second_end + counts[2]
    return (places >= first_end).astype(jnp.int32) + (places >= second_end).astype(jnp.int32) + (places >= third_end).astype(jnp.int32)

def attend_head(query_h, key_h, value_h, match_mask):
    raw_scores = low_back(jnp.dot(query_h, key_h.T, precision=precise))
    scores = jnp.where(match_mask, raw_scores * 0.125, -1000000000.0)
    maximum = lax.optimization_barrier(jnp.max(scores, axis=-1, keepdims=True))
    exp_terms = jnp.exp(scores - maximum)
    weights_soft = exp_terms / lax.optimization_barrier(jnp.sum(exp_terms, axis=-1, keepdims=True))
    return jnp.dot(low(weights_soft), value_h, precision=precise)

def split_heads(values):
    return values.reshape(values.shape[0], HEADS, HEAD).transpose(1, 0, 2)

def encode(inputs, seg_row, w_qkv, w_out, w_in, w_down, bias_query, bias_value, bias_out, gain_attn, shift_attn, bias_in, bias_down, gain_ffn, shift_ffn):
    projected = jnp.dot(inputs, w_qkv, precision=precise)
    query = low_back(low(projected[:, :D] + bias_query))
    key_all = low_back(low(projected[:, D:2 * D]))
    value_all = low_back(low(projected[:, 2 * D:] + bias_value))
    match_mask = seg_row[:, None] == seg_row[None, :]

    def one_head(items):
        return attend_head(items[0], items[1], items[2], match_mask)
    mixed = lax.map(jax.checkpoint(one_head), (split_heads(query), split_heads(key_all), split_heads(value_all)))
    context = low_back(low(mixed.transpose(1, 0, 2).reshape(inputs.shape[0], D)))
    attn_out = low_back(jnp.dot(context, w_out, precision=precise) + bias_out)
    hidden = layer_norm(inputs + attn_out, gain_attn, shift_attn)
    gate = low_back(jnp.dot(low(hidden), w_in, precision=precise) + bias_in)
    active = low(jax.nn.gelu(gate, approximate=False))
    ffn_out = low_back(jnp.dot(active, w_down, precision=precise) + bias_down)
    return layer_norm(hidden + ffn_out, gain_ffn, shift_ffn)

def reference(tokens, cotangent, doc_lengths, w_qkv, w_out, w_in, w_down, bias_query, bias_value, bias_out, gain_attn, shift_attn, bias_in, bias_down, gain_ffn, shift_ffn):
    params = tuple((piece.astype(jnp.float32) for piece in (w_qkv, w_out, w_in, w_down, bias_query, bias_value, bias_out, gain_attn, shift_attn, bias_in, bias_down, gain_ffn, shift_ffn)))
    seg_all = jax.vmap(lambda counts: segment_ids(counts, SEQ_LEN))(doc_lengths)

    def forward(inputs, *weights):

        def one_sequence(items):
            return jax.checkpoint(encode)(items[0], items[1], *weights)
        return lax.map(one_sequence, (inputs, seg_all))
    result, backward = jax.vjp(forward, tokens.astype(jnp.float32), *params)
    grads = backward(cotangent.astype(jnp.float32))
    return (result.astype(jnp.bfloat16), grads[0], grads[1], grads[2], grads[3], grads[4], grads[5], grads[6], grads[7], grads[8], grads[9], grads[10], grads[11], grads[12], grads[13])
```

```python
import functools

import jax
import jax.numpy as jnp
from jax import lax
from jax.experimental import pallas as pl
from jax.experimental.pallas import tpu as pltpu
from jax.sharding import PartitionSpec as P

HEADS = 12
HEAD = 64


epsilon = 1e-12
scale_attn = 0.125


def layer_norm(values, gain, shift):
    center = values - jnp.mean(values, axis=-1, keepdims=True)
    spread = jnp.mean(center * center, axis=-1, keepdims=True)
    return center * lax.rsqrt(spread + epsilon) * gain + shift


def gelu_exact(values):
    return jax.nn.gelu(values, approximate=False)


def segment_ids(counts, length):
    places = jnp.arange(length, dtype=jnp.int32)
    first_end = counts[0]
    second_end = first_end + counts[1]
    third_end = second_end + counts[2]
    return (
        (places >= first_end).astype(jnp.int32)
        + (places >= second_end).astype(jnp.int32)
        + (places >= third_end).astype(jnp.int32)
    )


def split_heads(values):
    return values.reshape(values.shape[0], HEADS, HEAD).transpose(1, 0, 2)


def join_heads(values):
    return values.transpose(1, 0, 2).reshape(values.shape[1], HEADS * HEAD)


def head_forward(query_h, key_h, value_h, match_mask):
    scores = (
        jnp.einsum("qd,kd->qk", query_h, key_h, preferred_element_type=jnp.float32) * scale_attn
    )
    scores = jnp.where(match_mask, scores, -1000000000.0)
    maximum = jnp.max(scores, axis=-1, keepdims=True)
    exp_terms = jnp.exp(scores - maximum)
    total = jnp.sum(exp_terms, axis=-1, keepdims=True)
    weights_soft = (exp_terms / total).astype(jnp.bfloat16)
    mixed = jnp.dot(weights_soft, value_h, preferred_element_type=jnp.float32)
    return (mixed, (maximum + jnp.log(total))[:, 0])


def head_backward(query_h, key_h, value_h, dctx_h, log_total, match_mask):
    scores = (
        jnp.einsum("qd,kd->qk", query_h, key_h, preferred_element_type=jnp.float32) * scale_attn
    )
    probs = jnp.where(match_mask, jnp.exp(scores - log_total[:, None]), 0.0)
    grad_probs = jnp.einsum("qd,kd->qk", dctx_h, value_h, preferred_element_type=jnp.float32)
    grad_value = jnp.einsum(
        "qk,qd->kd", probs.astype(jnp.bfloat16), dctx_h, preferred_element_type=jnp.float32
    )
    inner = jnp.sum(probs * grad_probs, axis=-1, keepdims=True)
    grad_scores = (probs * (grad_probs - inner) * scale_attn).astype(jnp.bfloat16)
    grad_query = jnp.dot(grad_scores, key_h, preferred_element_type=jnp.float32)
    grad_key = jnp.einsum("qk,qd->kd", grad_scores, query_h, preferred_element_type=jnp.float32)
    return (grad_query, grad_key, grad_value)


def column_sums(values):
    return jnp.sum(values.astype(jnp.float32), axis=0)


def local_any(
    tokens,
    cotangent,
    doc_lengths,
    w_qkv,
    w_out,
    w_in,
    w_down,
    bias_query,
    bias_value,
    bias_out,
    gain_attn,
    shift_attn,
    bias_in,
    bias_down,
    gain_ffn,
    shift_ffn,
):
    gathered = (
        lax.all_gather(w_qkv, "shard", axis=0, tiled=True),
        lax.all_gather(w_out, "shard", axis=0, tiled=True),
        lax.all_gather(w_in, "shard", axis=0, tiled=True),
        lax.all_gather(w_down, "shard", axis=0, tiled=True),
        lax.all_gather(bias_query, "shard", axis=0, tiled=True),
        lax.all_gather(bias_value, "shard", axis=0, tiled=True),
        lax.all_gather(bias_out, "shard", axis=0, tiled=True),
        lax.all_gather(gain_attn, "shard", axis=0, tiled=True),
        lax.all_gather(shift_attn, "shard", axis=0, tiled=True),
        lax.all_gather(bias_in, "shard", axis=0, tiled=True),
        lax.all_gather(bias_down, "shard", axis=0, tiled=True),
        lax.all_gather(gain_ffn, "shard", axis=0, tiled=True),
        lax.all_gather(shift_ffn, "shard", axis=0, tiled=True),
    )
    mat_qkv, mat_out, mat_in, mat_down = (gathered[0], gathered[1], gathered[2], gathered[3])
    vec_query, vec_value, vec_out, gain_a, shift_a, vec_in, vec_down, gain_f, shift_f = [
        piece.astype(jnp.float32) for piece in gathered[4:]
    ]
    rows = tokens.shape[1]
    width = tokens.shape[2]
    inputs = tokens[0]
    length = rows * lax.axis_size("ctx")
    all_ids = segment_ids(doc_lengths[0], length)
    own_ids = lax.dynamic_slice_in_dim(all_ids, lax.axis_index("ctx") * rows, rows)
    match_mask = own_ids[:, None] == all_ids[None, :]
    projected = jnp.dot(inputs, mat_qkv, preferred_element_type=jnp.float32)
    query = (projected[:, :width] + vec_query).astype(jnp.bfloat16)
    key_local = projected[:, width : 2 * width].astype(jnp.bfloat16)
    value_local = (projected[:, 2 * width :] + vec_value).astype(jnp.bfloat16)
    key_all, value_all = (
        lax.all_gather(key_local, "ctx", axis=0, tiled=True),
        lax.all_gather(value_local, "ctx", axis=0, tiled=True),
    )
    query_heads = split_heads(query)
    key_heads = split_heads(key_all)
    value_heads = split_heads(value_all)
    mixed, log_total = lax.map(
        lambda items: head_forward(items[0], items[1], items[2], match_mask),
        (query_heads, key_heads, value_heads),
    )
    context = join_heads(mixed).astype(jnp.bfloat16)
    resid_attn = inputs.astype(jnp.float32) + (
        jnp.dot(context, mat_out, preferred_element_type=jnp.float32) + vec_out
    )
    hidden = layer_norm(resid_attn, gain_a, shift_a)
    hidden_low = hidden.astype(jnp.bfloat16)
    gate = jnp.dot(hidden_low, mat_in, preferred_element_type=jnp.float32) + vec_in
    active = gelu_exact(gate).astype(jnp.bfloat16)
    resid_ffn = hidden + (jnp.dot(active, mat_down, preferred_element_type=jnp.float32) + vec_down)
    layer_out = layer_norm(resid_ffn, gain_f, shift_f).astype(jnp.bfloat16)
    regathered = (
        lax.all_gather(w_qkv, "shard", axis=0, tiled=True),
        lax.all_gather(w_out, "shard", axis=0, tiled=True),
        lax.all_gather(w_in, "shard", axis=0, tiled=True),
        lax.all_gather(w_down, "shard", axis=0, tiled=True),
    )
    mat_qkv, mat_out, mat_in, mat_down = (
        regathered[0],
        regathered[1],
        regathered[2],
        regathered[3],
    )
    upstream = cotangent[0].astype(jnp.float32)
    _, norm_ffn_back = jax.vjp(layer_norm, resid_ffn, gain_f, shift_f)
    grad_resid_ffn, g_gain_f, g_shift_f = norm_ffn_back(upstream)
    d_ffn = grad_resid_ffn.astype(jnp.bfloat16)
    g_down = jnp.einsum("tf,td->fd", active, d_ffn, preferred_element_type=jnp.float32)
    g_bdown = column_sums(d_ffn)
    d_active = jnp.einsum("td,fd->tf", d_ffn, mat_down, preferred_element_type=jnp.float32)
    _, gelu_back = jax.vjp(gelu_exact, gate)
    d_gate = gelu_back(d_active)[0].astype(jnp.bfloat16)
    g_in = jnp.einsum("td,tf->df", hidden_low, d_gate, preferred_element_type=jnp.float32)
    g_bin = column_sums(d_gate)
    d_hidden = grad_resid_ffn + jnp.einsum(
        "tf,df->td", d_gate, mat_in, preferred_element_type=jnp.float32
    )
    _, norm_attn_back = jax.vjp(layer_norm, resid_attn, gain_a, shift_a)
    grad_resid_attn, g_gain_a, g_shift_a = norm_attn_back(d_hidden)
    d_attn = grad_resid_attn.astype(jnp.bfloat16)
    g_out = jnp.einsum("tc,td->cd", context, d_attn, preferred_element_type=jnp.float32)
    g_bout = column_sums(d_attn)
    d_context = jnp.einsum("td,cd->tc", d_attn, mat_out, preferred_element_type=jnp.float32).astype(
        jnp.bfloat16
    )
    dctx_heads = split_heads(d_context)
    grad_query, grad_key, grad_value = lax.map(
        lambda items: head_backward(items[0], items[1], items[2], items[3], items[4], match_mask),
        (query_heads, key_heads, value_heads, dctx_heads, log_total),
    )
    key_terms = join_heads(grad_key)
    value_terms = join_heads(grad_value)
    key_summed, value_summed = (
        lax.psum_scatter(
            key_terms.astype(jnp.bfloat16), "ctx", scatter_dimension=0, tiled=True
        ).astype(jnp.float32),
        lax.psum_scatter(
            value_terms.astype(jnp.bfloat16), "ctx", scatter_dimension=0, tiled=True
        ).astype(jnp.float32),
    )
    d_query = join_heads(grad_query).astype(jnp.bfloat16)
    d_key = key_summed.astype(jnp.bfloat16)
    d_value = value_summed.astype(jnp.bfloat16)
    d_proj = jnp.concatenate([d_query, d_key, d_value], axis=1)
    g_qkv = jnp.einsum("td,te->de", inputs, d_proj, preferred_element_type=jnp.float32)
    g_query = column_sums(d_query)
    g_value = column_sums(d_value)
    grad_tokens = grad_resid_attn + jnp.einsum(
        "te,de->td", d_proj, mat_qkv, preferred_element_type=jnp.float32
    )
    group_parts = (
        lax.psum_scatter(
            g_qkv.astype(jnp.bfloat16), "shard", scatter_dimension=0, tiled=True
        ).astype(jnp.float32),
        lax.psum_scatter(
            g_out.astype(jnp.bfloat16), "shard", scatter_dimension=0, tiled=True
        ).astype(jnp.float32),
        lax.psum_scatter(
            g_in.astype(jnp.bfloat16), "shard", scatter_dimension=0, tiled=True
        ).astype(jnp.float32),
        lax.psum_scatter(
            g_down.astype(jnp.bfloat16), "shard", scatter_dimension=0, tiled=True
        ).astype(jnp.float32),
        lax.psum_scatter(
            g_query.astype(jnp.bfloat16), "shard", scatter_dimension=0, tiled=True
        ).astype(jnp.float32),
        lax.psum_scatter(
            g_value.astype(jnp.bfloat16), "shard", scatter_dimension=0, tiled=True
        ).astype(jnp.float32),
        lax.psum_scatter(
            g_bout.astype(jnp.bfloat16), "shard", scatter_dimension=0, tiled=True
        ).astype(jnp.float32),
        lax.psum_scatter(
            g_gain_a.astype(jnp.bfloat16), "shard", scatter_dimension=0, tiled=True
        ).astype(jnp.float32),
        lax.psum_scatter(
            g_shift_a.astype(jnp.bfloat16), "shard", scatter_dimension=0, tiled=True
        ).astype(jnp.float32),
        lax.psum_scatter(
            g_bin.astype(jnp.bfloat16), "shard", scatter_dimension=0, tiled=True
        ).astype(jnp.float32),
        lax.psum_scatter(
            g_bdown.astype(jnp.bfloat16), "shard", scatter_dimension=0, tiled=True
        ).astype(jnp.float32),
        lax.psum_scatter(
            g_gain_f.astype(jnp.bfloat16), "shard", scatter_dimension=0, tiled=True
        ).astype(jnp.float32),
        lax.psum_scatter(
            g_shift_f.astype(jnp.bfloat16), "shard", scatter_dimension=0, tiled=True
        ).astype(jnp.float32),
    )
    (
        p_qkv,
        p_out,
        p_in,
        p_down,
        p_query,
        p_value,
        p_bout,
        p_gain_a,
        p_shift_a,
        p_bin,
        p_bdown,
        p_gain_f,
        p_shift_f,
    ) = group_parts
    summed = (
        lax.psum(p_qkv.astype(jnp.bfloat16), "ctx").astype(jnp.float32),
        lax.psum(p_out.astype(jnp.bfloat16), "ctx").astype(jnp.float32),
        lax.psum(p_in.astype(jnp.bfloat16), "ctx").astype(jnp.float32),
        lax.psum(p_down.astype(jnp.bfloat16), "ctx").astype(jnp.float32),
        lax.psum(p_query.astype(jnp.bfloat16), "ctx").astype(jnp.float32),
        lax.psum(p_value.astype(jnp.bfloat16), "ctx").astype(jnp.float32),
        lax.psum(p_bout.astype(jnp.bfloat16), "ctx").astype(jnp.float32),
        lax.psum(p_gain_a.astype(jnp.bfloat16), "ctx").astype(jnp.float32),
        lax.psum(p_shift_a.astype(jnp.bfloat16), "ctx").astype(jnp.float32),
        lax.psum(p_bin.astype(jnp.bfloat16), "ctx").astype(jnp.float32),
        lax.psum(p_bdown.astype(jnp.bfloat16), "ctx").astype(jnp.float32),
        lax.psum(p_gain_f.astype(jnp.bfloat16), "ctx").astype(jnp.float32),
        lax.psum(p_shift_f.astype(jnp.bfloat16), "ctx").astype(jnp.float32),
    )
    return (
        layer_out[None],
        grad_tokens[None],
        summed[0],
        summed[1],
        summed[2],
        summed[3],
        summed[4],
        summed[5],
        summed[6],
        summed[7],
        summed[8],
        summed[9],
        summed[10],
        summed[11],
        summed[12],
    )


QUERY_BLOCK = 256
VMEM_BYTES = 56 * 1024 * 1024
TN = (((0,), (0,)), ((), ()))
NT = (((1,), (1,)), ((), ()))


def dot(a, b, dims=(((1,), (0,)), ((), ()))):
    return lax.dot_general(a, b, dims, preferred_element_type=jnp.float32)


def attend_kernel(ids_row, ids_col, q_ref, k_ref, v_ref, ctx_ref, p_ref):
    scores = dot(k_ref[...], q_ref[...] * jnp.bfloat16(0.125), TN)
    scores = jnp.where(ids_col[...] == ids_row[...], scores, -1000000000.0)
    maximum = jnp.max(scores, axis=0, keepdims=True)
    terms = jnp.exp(scores - maximum)
    total = jnp.sum(terms, axis=0, keepdims=True)
    probs = (terms * (1.0 / total)).astype(jnp.bfloat16)
    p_ref[0] = probs
    ctx_ref[...] = dot(v_ref[...], probs).astype(jnp.bfloat16)


def attend(ids, q, k, v):
    width, length = q.shape
    heads = width // HEAD
    block = QUERY_BLOCK
    row = pl.BlockSpec((HEAD, length), lambda h, b: (h, 0))
    part = pl.BlockSpec((HEAD, block), lambda h, b: (h, b))
    return pl.pallas_call(
        attend_kernel,
        grid=(heads, length // block),
        in_specs=[
            pl.BlockSpec((1, block), lambda h, b: (0, b)),
            pl.BlockSpec((length, 1), lambda h, b: (0, 0)),
            part,
            row,
            row,
        ],
        out_specs=[part, pl.BlockSpec((1, length, block), lambda h, b: (h, 0, b))],
        out_shape=[
            jax.ShapeDtypeStruct((width, length), jnp.bfloat16),
            jax.ShapeDtypeStruct((heads, length, length), jnp.bfloat16),
        ],
        compiler_params=pltpu.CompilerParams(vmem_limit_bytes=VMEM_BYTES),
        cost_estimate=pl.CostEstimate(
            flops=heads * length * length * 256 * 4,
            bytes_accessed=heads * length * length * 4,
            transcendentals=heads * length * length,
        ),
        name="attend",
    )(ids[None, :], ids[:, None], q, k, v)


def attend_back_kernel(
    q_ref, k_ref, v_ref, d_ref, ctx_ref, p_ref, dq_ref, dk_ref, dv_ref, dk_sum, dv_sum
):
    step = pl.program_id(1)

    @pl.when(step == 0)
    def _():
        dk_sum[...] = jnp.zeros_like(dk_sum)
        dv_sum[...] = jnp.zeros_like(dv_sum)

    probs = p_ref[0]
    d_ctx = d_ref[...]
    inner = jnp.sum(
        d_ctx.astype(jnp.float32) * ctx_ref[...].astype(jnp.float32), axis=0, keepdims=True
    )
    d_probs = dot(v_ref[...], d_ctx, TN)
    d_scores = (probs.astype(jnp.float32) * (d_probs - inner)).astype(jnp.bfloat16)
    dq_ref[...] = (dot(k_ref[...], d_scores) * 0.125).astype(jnp.bfloat16)
    dk_sum[...] += dot(d_scores, q_ref[...], NT)
    dv_sum[...] += dot(probs, d_ctx, NT)

    @pl.when(step == pl.num_programs(1) - 1)
    def _():
        dk_ref[...] = (dk_sum[...].T * 0.125).astype(jnp.bfloat16)
        dv_ref[...] = dv_sum[...].T.astype(jnp.bfloat16)


def attend_back(q, k, v, d_ctx, ctx, probs):
    width, length = q.shape
    heads = width // HEAD
    block = QUERY_BLOCK
    row = pl.BlockSpec((HEAD, length), lambda h, b: (h, 0))
    part = pl.BlockSpec((HEAD, block), lambda h, b: (h, b))
    shape = jax.ShapeDtypeStruct((width, length), jnp.bfloat16)
    return pl.pallas_call(
        attend_back_kernel,
        grid=(heads, length // block),
        in_specs=[
            part,
            row,
            row,
            part,
            part,
            pl.BlockSpec((1, length, block), lambda h, b: (h, 0, b)),
        ],
        out_specs=[part, row, row],
        out_shape=[shape, shape, shape],
        scratch_shapes=[pltpu.VMEM((length, HEAD), jnp.float32)] * 2,
        compiler_params=pltpu.CompilerParams(vmem_limit_bytes=VMEM_BYTES),
        cost_estimate=pl.CostEstimate(
            flops=heads * length * length * 256 * 10,
            bytes_accessed=heads * length * length * 4,
            transcendentals=0,
        ),
        name="attend_back",
    )(q, k, v, d_ctx, ctx, probs)


def swap(values, bit):
    return lax.ppermute(values, "shard", [(i, i ^ bit) for i in range(8)])


def place_kernel(*refs):
    *pieces, whole, sems = refs
    me = lax.axis_index("shard")
    rows = pieces[0].shape[0]
    half = rows // 2
    copies = []
    for core in (0, 1):
        own, over_x, over_y, top, bottom = pieces[core * 5 : core * 5 + 5]
        for piece, bits, shift in (
            (own, 0, 0),
            (over_x, 2, 0),
            (over_y, 4, 0),
            (top, 6, 0),
            (bottom, 6, half),
        ):
            owner = flip(me, bits + core)
            start = pl.multiple_of(owner * rows + shift, 16)
            copies.append(
                pltpu.make_async_copy(
                    piece, whole.at[pl.ds(start, piece.shape[0])], sems.at[len(copies)]
                )
            )
    for copy in copies:
        copy.start()
    for copy in copies:
        copy.wait()


def flip(index, bits):
    result = index
    for bit in (1, 2, 4):
        if bits & bit:
            held = lax.rem(index // bit, 2)
            result = result + bit - 2 * bit * held
    return result


def gather_shard(piece):
    rows, columns = piece.shape
    half = rows // 2
    over_x = swap(piece, 2)
    over_y = swap(piece, 4)
    top = swap(over_x[:half], 4)
    bottom = swap(over_y[half:], 2)
    near = [piece, over_x, over_y, top, bottom]
    far = [swap(part, 1) for part in near]
    return pl.pallas_call(
        place_kernel,
        in_specs=[pl.BlockSpec(memory_space=pl.ANY)] * 10,
        out_specs=pl.BlockSpec(memory_space=pl.ANY),
        out_shape=jax.ShapeDtypeStruct((8 * rows, columns), piece.dtype),
        scratch_shapes=[pltpu.SemaphoreType.DMA((10,))],
        cost_estimate=pl.CostEstimate(
            flops=0, bytes_accessed=32 * rows * columns, transcendentals=0
        ),
        name="place_rows",
    )(*near, *far)


def add_low(a, b):
    return (a.astype(jnp.float32) + b.astype(jnp.float32)).astype(jnp.bfloat16)


def pick(values, index, axis):
    return lax.dynamic_index_in_dim(values, index, axis, keepdims=False)


def scatter_shard(whole):
    me = lax.axis_index("shard")
    core, x, y = me % 2, (me // 2) % 2, me // 4
    rows, columns = whole.shape[0] // 8, whole.shape[1]
    half = columns // 2
    parts = whole.reshape(4, 2, rows, columns)
    mine = add_low(pick(parts, core, 1), swap(pick(parts, 1 - core, 1), 1))
    mine = mine.reshape(2, 2, rows, columns)
    left, right = mine[..., :half], mine[..., half:]
    left = add_low(pick(left, x, 1), swap(pick(left, 1 - x, 1), 2))
    right = add_low(pick(right, y, 0), swap(pick(right, 1 - y, 0), 4))
    left = add_low(pick(left, y, 0), swap(pick(left, 1 - y, 0), 4))
    right = add_low(pick(right, x, 0), swap(pick(right, 1 - x, 0), 2))
    return jnp.concatenate([left, right], axis=1)


def local_fast(
    tokens,
    cotangent,
    doc_lengths,
    w_qkv,
    w_out,
    w_in,
    w_down,
    bias_query,
    bias_value,
    bias_out,
    gain_attn,
    shift_attn,
    bias_in,
    bias_down,
    gain_ffn,
    shift_ffn,
):
    blocks = lax.axis_size("ctx")
    place = lax.axis_index("ctx")
    inputs = tokens[0]
    rows, width = inputs.shape
    length = rows * blocks
    share = width // blocks
    vectors = [
        bias_query,
        bias_value,
        bias_out,
        gain_attn,
        shift_attn,
        bias_in,
        bias_down,
        gain_ffn,
        shift_ffn,
    ]
    sizes = [vector.shape[0] for vector in vectors]

    tokens_all = lax.all_gather(inputs, "ctx", axis=0, tiled=True)
    qkv_part = lax.dynamic_index_in_dim(
        w_qkv.reshape(w_qkv.shape[0], 3, blocks, share), place, 2, keepdims=False
    ).reshape(w_qkv.shape[0], 3 * share)
    mat_qkv = gather_shard(qkv_part)
    packed = lax.all_gather(jnp.concatenate(vectors), "shard", axis=0, tiled=False)
    mat_out = gather_shard(w_out)
    mat_in = gather_shard(w_in)
    mat_down = gather_shard(w_down)
    edges = [sum(sizes[:i]) for i in range(len(sizes) + 1)]
    vec_query, vec_value, vec_out, gain_a, shift_a, vec_in, vec_down, gain_f, shift_f = [
        packed[:, edges[i] : edges[i + 1]].reshape(-1).astype(jnp.float32)
        for i in range(len(sizes))
    ]

    ids = segment_ids(doc_lengths[0], length)
    bias_q = lax.dynamic_slice_in_dim(vec_query, place * share, share)
    bias_v = lax.dynamic_slice_in_dim(vec_value, place * share, share)
    proj = lax.dot_general(
        mat_qkv, tokens_all, (((0,), (1,)), ((), ())), preferred_element_type=jnp.float32
    )
    query = (proj[:share] + bias_q[:, None]).astype(jnp.bfloat16)
    key = proj[share : 2 * share].astype(jnp.bfloat16)
    value = (proj[2 * share :] + bias_v[:, None]).astype(jnp.bfloat16)
    mixed, probs = attend(ids, query, key, value)
    context = lax.all_to_all(mixed, "ctx", 1, 0, tiled=True)

    resid_attn = inputs.astype(jnp.float32) + (dot(context, mat_out, TN) + vec_out)
    hidden = layer_norm(resid_attn, gain_a, shift_a)
    hidden_low = hidden.astype(jnp.bfloat16)
    gate = dot(hidden_low, mat_in) + vec_in
    active = gelu_exact(gate).astype(jnp.bfloat16)
    resid_ffn = hidden + (dot(active, mat_down) + vec_down)
    layer_out = layer_norm(resid_ffn, gain_f, shift_f).astype(jnp.bfloat16)

    upstream = cotangent[0].astype(jnp.float32)
    _, norm_ffn_back = jax.vjp(layer_norm, resid_ffn, gain_f, shift_f)
    grad_resid_ffn, g_gain_f, g_shift_f = norm_ffn_back(upstream)
    d_ffn = grad_resid_ffn.astype(jnp.bfloat16)
    g_down = dot(active, d_ffn, TN).astype(jnp.bfloat16)
    g_bdown = column_sums(d_ffn)
    d_active = dot(d_ffn, mat_down, NT)
    _, gelu_back = jax.vjp(gelu_exact, gate)
    d_gate = gelu_back(d_active)[0].astype(jnp.bfloat16)
    g_in = dot(hidden_low, d_gate, TN).astype(jnp.bfloat16)
    g_bin = column_sums(d_gate)
    d_hidden = grad_resid_ffn + dot(d_gate, mat_in, NT)
    _, norm_attn_back = jax.vjp(layer_norm, resid_attn, gain_a, shift_a)
    grad_resid_attn, g_gain_a, g_shift_a = norm_attn_back(d_hidden)
    d_attn = grad_resid_attn.astype(jnp.bfloat16)
    g_out = dot(context, d_attn).astype(jnp.bfloat16)
    g_bout = column_sums(d_attn)
    d_context = dot(mat_out, d_attn, NT).astype(jnp.bfloat16)

    d_context, g_down, g_in, g_out = lax.optimization_barrier((d_context, g_down, g_in, g_out))
    d_mixed = lax.all_to_all(d_context, "ctx", 0, 1, tiled=True)
    s_down = scatter_shard(g_down)
    s_in = scatter_shard(g_in)
    s_out = scatter_shard(g_out)
    d_query, d_key, d_value = attend_back(query, key, value, d_mixed, mixed, probs)
    d_proj = jnp.concatenate([d_query, d_key, d_value], axis=0)
    spread = dot(d_proj, mat_qkv, (((0,), (1,)), ((), ()))).astype(jnp.bfloat16)
    summed_tokens = lax.psum_scatter(spread, "ctx", scatter_dimension=0, tiled=True)
    grad_tokens = grad_resid_attn + summed_tokens.astype(jnp.float32)
    g_qkv = lax.dot_general(
        tokens_all, d_proj, (((0,), (1,)), ((), ())), preferred_element_type=jnp.float32
    ).astype(jnp.bfloat16)
    s_qkv = scatter_shard(g_qkv)
    all_qkv = lax.all_gather(s_qkv.reshape(-1, 3, share), "ctx", axis=2, tiled=True)
    out_qkv = all_qkv.reshape(-1, 3 * width).astype(jnp.float32)

    def widen(part):
        whole = jnp.zeros((width,), jnp.float32)
        return lax.dynamic_update_slice_in_dim(whole, part, place * share, 0)

    g_query = widen(jnp.sum(d_query.astype(jnp.float32), axis=1))
    g_value = widen(jnp.sum(d_value.astype(jnp.float32), axis=1))
    small = [g_query, g_value, g_bout, g_gain_a, g_shift_a, g_bin, g_bdown, g_gain_f, g_shift_f]
    small = jnp.concatenate([part.reshape(8, -1) for part in small], axis=1)
    small = lax.psum(small, ("shard", "ctx"))
    small = lax.dynamic_index_in_dim(small, lax.axis_index("shard"), 0, keepdims=False)
    small = [small[edges[i] : edges[i + 1]] for i in range(len(sizes))]
    out_down = lax.psum(s_down, "ctx").astype(jnp.float32)
    out_in = lax.psum(s_in, "ctx").astype(jnp.float32)
    out_out = lax.psum(s_out, "ctx").astype(jnp.float32)
    return (
        layer_out[None],
        grad_tokens[None],
        out_qkv,
        out_out,
        out_in,
        out_down,
        *small,
    )


def solution(mesh):
    sizes = (mesh.shape["shard"], mesh.shape["ctx"])
    chosen = local_fast if sizes == (8, 4) else local_any
    return jax.shard_map(
        chosen,
        mesh=mesh,
        in_specs=(
            P("shard", "ctx", None),
            P("shard", "ctx", None),
            P("shard", None),
            P("shard", None),
            P("shard", None),
            P("shard", None),
            P("shard", None),
            P("shard"),
            P("shard"),
            P("shard"),
            P("shard"),
            P("shard"),
            P("shard"),
            P("shard"),
            P("shard"),
            P("shard"),
        ),
        out_specs=(
            P("shard", "ctx", None),
            P("shard", "ctx", None),
            P("shard", None),
            P("shard", None),
            P("shard", None),
            P("shard", None),
            P("shard"),
            P("shard"),
            P("shard"),
            P("shard"),
            P("shard"),
            P("shard"),
            P("shard"),
            P("shard"),
            P("shard"),
        ),
        check_vma=False,
    )
```

```python
import functools

import jax
import jax.numpy as jnp
from jax import lax
from jax.experimental import pallas as pl
from jax.experimental.pallas import tpu as pltpu
from jax.sharding import PartitionSpec as P

HEADS = 12
HEAD = 64


epsilon = 1e-12
scale_attn = 0.125


def layer_norm(values, gain, shift):
    center = values - jnp.mean(values, axis=-1, keepdims=True)
    spread = jnp.mean(center * center, axis=-1, keepdims=True)
    return center * lax.rsqrt(spread + epsilon) * gain + shift


def gelu_exact(values):
    return jax.nn.gelu(values, approximate=False)


def segment_ids(counts, length):
    places = jnp.arange(length, dtype=jnp.int32)
    first_end = counts[0]
    second_end = first_end + counts[1]
    third_end = second_end + counts[2]
    return (
        (places >= first_end).astype(jnp.int32)
        + (places >= second_end).astype(jnp.int32)
        + (places >= third_end).astype(jnp.int32)
    )


def split_heads(values):
    return values.reshape(values.shape[0], HEADS, HEAD).transpose(1, 0, 2)


def join_heads(values):
    return values.transpose(1, 0, 2).reshape(values.shape[1], HEADS * HEAD)


def head_forward(query_h, key_h, value_h, match_mask):
    scores = (
        jnp.einsum("qd,kd->qk", query_h, key_h, preferred_element_type=jnp.float32) * scale_attn
    )
    scores = jnp.where(match_mask, scores, -1000000000.0)
    maximum = jnp.max(scores, axis=-1, keepdims=True)
    exp_terms = jnp.exp(scores - maximum)
    total = jnp.sum(exp_terms, axis=-1, keepdims=True)
    weights_soft = (exp_terms / total).astype(jnp.bfloat16)
    mixed = jnp.dot(weights_soft, value_h, preferred_element_type=jnp.float32)
    return (mixed, (maximum + jnp.log(total))[:, 0])


def head_backward(query_h, key_h, value_h, dctx_h, log_total, match_mask):
    scores = (
        jnp.einsum("qd,kd->qk", query_h, key_h, preferred_element_type=jnp.float32) * scale_attn
    )
    probs = jnp.where(match_mask, jnp.exp(scores - log_total[:, None]), 0.0)
    grad_probs = jnp.einsum("qd,kd->qk", dctx_h, value_h, preferred_element_type=jnp.float32)
    grad_value = jnp.einsum(
        "qk,qd->kd", probs.astype(jnp.bfloat16), dctx_h, preferred_element_type=jnp.float32
    )
    inner = jnp.sum(probs * grad_probs, axis=-1, keepdims=True)
    grad_scores = (probs * (grad_probs - inner) * scale_attn).astype(jnp.bfloat16)
    grad_query = jnp.dot(grad_scores, key_h, preferred_element_type=jnp.float32)
    grad_key = jnp.einsum("qk,qd->kd", grad_scores, query_h, preferred_element_type=jnp.float32)
    return (grad_query, grad_key, grad_value)


def column_sums(values):
    return jnp.sum(values.astype(jnp.float32), axis=0)


def local_any(
    tokens,
    cotangent,
    doc_lengths,
    w_qkv,
    w_out,
    w_in,
    w_down,
    bias_query,
    bias_value,
    bias_out,
    gain_attn,
    shift_attn,
    bias_in,
    bias_down,
    gain_ffn,
    shift_ffn,
):
    gathered = (
        lax.all_gather(w_qkv, "shard", axis=0, tiled=True),
        lax.all_gather(w_out, "shard", axis=0, tiled=True),
        lax.all_gather(w_in, "shard", axis=0, tiled=True),
        lax.all_gather(w_down, "shard", axis=0, tiled=True),
        lax.all_gather(bias_query, "shard", axis=0, tiled=True),
        lax.all_gather(bias_value, "shard", axis=0, tiled=True),
        lax.all_gather(bias_out, "shard", axis=0, tiled=True),
        lax.all_gather(gain_attn, "shard", axis=0, tiled=True),
        lax.all_gather(shift_attn, "shard", axis=0, tiled=True),
        lax.all_gather(bias_in, "shard", axis=0, tiled=True),
        lax.all_gather(bias_down, "shard", axis=0, tiled=True),
        lax.all_gather(gain_ffn, "shard", axis=0, tiled=True),
        lax.all_gather(shift_ffn, "shard", axis=0, tiled=True),
    )
    mat_qkv, mat_out, mat_in, mat_down = (gathered[0], gathered[1], gathered[2], gathered[3])
    vec_query, vec_value, vec_out, gain_a, shift_a, vec_in, vec_down, gain_f, shift_f = [
        piece.astype(jnp.float32) for piece in gathered[4:]
    ]
    rows = tokens.shape[1]
    width = tokens.shape[2]
    inputs = tokens[0]
    length = rows * lax.axis_size("ctx")
    all_ids = segment_ids(doc_lengths[0], length)
    own_ids = lax.dynamic_slice_in_dim(all_ids, lax.axis_index("ctx") * rows, rows)
    match_mask = own_ids[:, None] == all_ids[None, :]
    projected = jnp.dot(inputs, mat_qkv, preferred_element_type=jnp.float32)
    query = (projected[:, :width] + vec_query).astype(jnp.bfloat16)
    key_local = projected[:, width : 2 * width].astype(jnp.bfloat16)
    value_local = (projected[:, 2 * width :] + vec_value).astype(jnp.bfloat16)
    key_all, value_all = (
        lax.all_gather(key_local, "ctx", axis=0, tiled=True),
        lax.all_gather(value_local, "ctx", axis=0, tiled=True),
    )
    query_heads = split_heads(query)
    key_heads = split_heads(key_all)
    value_heads = split_heads(value_all)
    mixed, log_total = lax.map(
        lambda items: head_forward(items[0], items[1], items[2], match_mask),
        (query_heads, key_heads, value_heads),
    )
    context = join_heads(mixed).astype(jnp.bfloat16)
    resid_attn = inputs.astype(jnp.float32) + (
        jnp.dot(context, mat_out, preferred_element_type=jnp.float32) + vec_out
    )
    hidden = layer_norm(resid_attn, gain_a, shift_a)
    hidden_low = hidden.astype(jnp.bfloat16)
    gate = jnp.dot(hidden_low, mat_in, preferred_element_type=jnp.float32) + vec_in
    active = gelu_exact(gate).astype(jnp.bfloat16)
    resid_ffn = hidden + (jnp.dot(active, mat_down, preferred_element_type=jnp.float32) + vec_down)
    layer_out = layer_norm(resid_ffn, gain_f, shift_f).astype(jnp.bfloat16)
    regathered = (
        lax.all_gather(w_qkv, "shard", axis=0, tiled=True),
        lax.all_gather(w_out, "shard", axis=0, tiled=True),
        lax.all_gather(w_in, "shard", axis=0, tiled=True),
        lax.all_gather(w_down, "shard", axis=0, tiled=True),
    )
    mat_qkv, mat_out, mat_in, mat_down = (
        regathered[0],
        regathered[1],
        regathered[2],
        regathered[3],
    )
    upstream = cotangent[0].astype(jnp.float32)
    _, norm_ffn_back = jax.vjp(layer_norm, resid_ffn, gain_f, shift_f)
    grad_resid_ffn, g_gain_f, g_shift_f = norm_ffn_back(upstream)
    d_ffn = grad_resid_ffn.astype(jnp.bfloat16)
    g_down = jnp.einsum("tf,td->fd", active, d_ffn, preferred_element_type=jnp.float32)
    g_bdown = column_sums(d_ffn)
    d_active = jnp.einsum("td,fd->tf", d_ffn, mat_down, preferred_element_type=jnp.float32)
    _, gelu_back = jax.vjp(gelu_exact, gate)
    d_gate = gelu_back(d_active)[0].astype(jnp.bfloat16)
    g_in = jnp.einsum("td,tf->df", hidden_low, d_gate, preferred_element_type=jnp.float32)
    g_bin = column_sums(d_gate)
    d_hidden = grad_resid_ffn + jnp.einsum(
        "tf,df->td", d_gate, mat_in, preferred_element_type=jnp.float32
    )
    _, norm_attn_back = jax.vjp(layer_norm, resid_attn, gain_a, shift_a)
    grad_resid_attn, g_gain_a, g_shift_a = norm_attn_back(d_hidden)
    d_attn = grad_resid_attn.astype(jnp.bfloat16)
    g_out = jnp.einsum("tc,td->cd", context, d_attn, preferred_element_type=jnp.float32)
    g_bout = column_sums(d_attn)
    d_context = jnp.einsum("td,cd->tc", d_attn, mat_out, preferred_element_type=jnp.float32).astype(
        jnp.bfloat16
    )
    dctx_heads = split_heads(d_context)
    grad_query, grad_key, grad_value = lax.map(
        lambda items: head_backward(items[0], items[1], items[2], items[3], items[4], match_mask),
        (query_heads, key_heads, value_heads, dctx_heads, log_total),
    )
    key_terms = join_heads(grad_key)
    value_terms = join_heads(grad_value)
    key_summed, value_summed = (
        lax.psum_scatter(
            key_terms.astype(jnp.bfloat16), "ctx", scatter_dimension=0, tiled=True
        ).astype(jnp.float32),
        lax.psum_scatter(
            value_terms.astype(jnp.bfloat16), "ctx", scatter_dimension=0, tiled=True
        ).astype(jnp.float32),
    )
    d_query = join_heads(grad_query).astype(jnp.bfloat16)
    d_key = key_summed.astype(jnp.bfloat16)
    d_value = value_summed.astype(jnp.bfloat16)
    d_proj = jnp.concatenate([d_query, d_key, d_value], axis=1)
    g_qkv = jnp.einsum("td,te->de", inputs, d_proj, preferred_element_type=jnp.float32)
    g_query = column_sums(d_query)
    g_value = column_sums(d_value)
    grad_tokens = grad_resid_attn + jnp.einsum(
        "te,de->td", d_proj, mat_qkv, preferred_element_type=jnp.float32
    )
    group_parts = (
        lax.psum_scatter(
            g_qkv.astype(jnp.bfloat16), "shard", scatter_dimension=0, tiled=True
        ).astype(jnp.float32),
        lax.psum_scatter(
            g_out.astype(jnp.bfloat16), "shard", scatter_dimension=0, tiled=True
        ).astype(jnp.float32),
        lax.psum_scatter(
            g_in.astype(jnp.bfloat16), "shard", scatter_dimension=0, tiled=True
        ).astype(jnp.float32),
        lax.psum_scatter(
            g_down.astype(jnp.bfloat16), "shard", scatter_dimension=0, tiled=True
        ).astype(jnp.float32),
        lax.psum_scatter(
            g_query.astype(jnp.bfloat16), "shard", scatter_dimension=0, tiled=True
        ).astype(jnp.float32),
        lax.psum_scatter(
            g_value.astype(jnp.bfloat16), "shard", scatter_dimension=0, tiled=True
        ).astype(jnp.float32),
        lax.psum_scatter(
            g_bout.astype(jnp.bfloat16), "shard", scatter_dimension=0, tiled=True
        ).astype(jnp.float32),
        lax.psum_scatter(
            g_gain_a.astype(jnp.bfloat16), "shard", scatter_dimension=0, tiled=True
        ).astype(jnp.float32),
        lax.psum_scatter(
            g_shift_a.astype(jnp.bfloat16), "shard", scatter_dimension=0, tiled=True
        ).astype(jnp.float32),
        lax.psum_scatter(
            g_bin.astype(jnp.bfloat16), "shard", scatter_dimension=0, tiled=True
        ).astype(jnp.float32),
        lax.psum_scatter(
            g_bdown.astype(jnp.bfloat16), "shard", scatter_dimension=0, tiled=True
        ).astype(jnp.float32),
        lax.psum_scatter(
            g_gain_f.astype(jnp.bfloat16), "shard", scatter_dimension=0, tiled=True
        ).astype(jnp.float32),
        lax.psum_scatter(
            g_shift_f.astype(jnp.bfloat16), "shard", scatter_dimension=0, tiled=True
        ).astype(jnp.float32),
    )
    (
        p_qkv,
        p_out,
        p_in,
        p_down,
        p_query,
        p_value,
        p_bout,
        p_gain_a,
        p_shift_a,
        p_bin,
        p_bdown,
        p_gain_f,
        p_shift_f,
    ) = group_parts
    summed = (
        lax.psum(p_qkv.astype(jnp.bfloat16), "ctx").astype(jnp.float32),
        lax.psum(p_out.astype(jnp.bfloat16), "ctx").astype(jnp.float32),
        lax.psum(p_in.astype(jnp.bfloat16), "ctx").astype(jnp.float32),
        lax.psum(p_down.astype(jnp.bfloat16), "ctx").astype(jnp.float32),
        lax.psum(p_query.astype(jnp.bfloat16), "ctx").astype(jnp.float32),
        lax.psum(p_value.astype(jnp.bfloat16), "ctx").astype(jnp.float32),
        lax.psum(p_bout.astype(jnp.bfloat16), "ctx").astype(jnp.float32),
        lax.psum(p_gain_a.astype(jnp.bfloat16), "ctx").astype(jnp.float32),
        lax.psum(p_shift_a.astype(jnp.bfloat16), "ctx").astype(jnp.float32),
        lax.psum(p_bin.astype(jnp.bfloat16), "ctx").astype(jnp.float32),
        lax.psum(p_bdown.astype(jnp.bfloat16), "ctx").astype(jnp.float32),
        lax.psum(p_gain_f.astype(jnp.bfloat16), "ctx").astype(jnp.float32),
        lax.psum(p_shift_f.astype(jnp.bfloat16), "ctx").astype(jnp.float32),
    )
    return (
        layer_out[None],
        grad_tokens[None],
        summed[0],
        summed[1],
        summed[2],
        summed[3],
        summed[4],
        summed[5],
        summed[6],
        summed[7],
        summed[8],
        summed[9],
        summed[10],
        summed[11],
        summed[12],
    )


QUERY_BLOCK = 256
VMEM_BYTES = 56 * 1024 * 1024
TN = (((0,), (0,)), ((), ()))
NT = (((1,), (1,)), ((), ()))


def dot(a, b, dims=(((1,), (0,)), ((), ()))):
    return lax.dot_general(a, b, dims, preferred_element_type=jnp.float32)


def attend_kernel(ids_row, ids_col, q_ref, k_ref, v_ref, ctx_ref, p_ref):
    scores = dot(k_ref[...], q_ref[...] * jnp.bfloat16(0.125), TN)
    scores = jnp.where(ids_col[...] == ids_row[...], scores, -1000000000.0)
    maximum = jnp.max(scores, axis=0, keepdims=True)
    terms = jnp.exp(scores - maximum)
    total = jnp.sum(terms, axis=0, keepdims=True)
    probs = (terms * (1.0 / total)).astype(jnp.bfloat16)
    p_ref[0] = probs
    ctx_ref[...] = dot(v_ref[...], probs).astype(jnp.bfloat16)


def attend(ids, q, k, v):
    width, length = q.shape
    heads = width // HEAD
    block = QUERY_BLOCK
    row = pl.BlockSpec((HEAD, length), lambda h, b: (h, 0))
    part = pl.BlockSpec((HEAD, block), lambda h, b: (h, b))
    return pl.pallas_call(
        attend_kernel,
        grid=(heads, length // block),
        in_specs=[
            pl.BlockSpec((1, block), lambda h, b: (0, b)),
            pl.BlockSpec((length, 1), lambda h, b: (0, 0)),
            part,
            row,
            row,
        ],
        out_specs=[part, pl.BlockSpec((1, length, block), lambda h, b: (h, 0, b))],
        out_shape=[
            jax.ShapeDtypeStruct((width, length), jnp.bfloat16),
            jax.ShapeDtypeStruct((heads, length, length), jnp.bfloat16),
        ],
        compiler_params=pltpu.CompilerParams(vmem_limit_bytes=VMEM_BYTES),
        cost_estimate=pl.CostEstimate(
            flops=heads * length * length * 256 * 4,
            bytes_accessed=heads * length * length * 4,
            transcendentals=heads * length * length,
        ),
        name="attend",
    )(ids[None, :], ids[:, None], q, k, v)


def attend_back_kernel(
    q_ref, k_ref, v_ref, d_ref, ctx_ref, p_ref, dq_ref, dk_ref, dv_ref, dk_sum, dv_sum
):
    step = pl.program_id(1)

    @pl.when(step == 0)
    def _():
        dk_sum[...] = jnp.zeros_like(dk_sum)
        dv_sum[...] = jnp.zeros_like(dv_sum)

    probs = p_ref[0]
    d_ctx = d_ref[...]
    inner = jnp.sum(
        d_ctx.astype(jnp.float32) * ctx_ref[...].astype(jnp.float32), axis=0, keepdims=True
    )
    d_probs = dot(v_ref[...], d_ctx, TN)
    d_scores = (probs.astype(jnp.float32) * (d_probs - inner)).astype(jnp.bfloat16)
    dq_ref[...] = (dot(k_ref[...], d_scores) * 0.125).astype(jnp.bfloat16)
    dk_sum[...] += dot(d_scores, q_ref[...], NT)
    dv_sum[...] += dot(probs, d_ctx, NT)

    @pl.when(step == pl.num_programs(1) - 1)
    def _():
        dk_ref[...] = (dk_sum[...].T * 0.125).astype(jnp.bfloat16)
        dv_ref[...] = dv_sum[...].T.astype(jnp.bfloat16)


def attend_back(q, k, v, d_ctx, ctx, probs):
    width, length = q.shape
    heads = width // HEAD
    block = QUERY_BLOCK
    row = pl.BlockSpec((HEAD, length), lambda h, b: (h, 0))
    part = pl.BlockSpec((HEAD, block), lambda h, b: (h, b))
    shape = jax.ShapeDtypeStruct((width, length), jnp.bfloat16)
    return pl.pallas_call(
        attend_back_kernel,
        grid=(heads, length // block),
        in_specs=[
            part,
            row,
            row,
            part,
            part,
            pl.BlockSpec((1, length, block), lambda h, b: (h, 0, b)),
        ],
        out_specs=[part, row, row],
        out_shape=[shape, shape, shape],
        scratch_shapes=[pltpu.VMEM((length, HEAD), jnp.float32)] * 2,
        compiler_params=pltpu.CompilerParams(vmem_limit_bytes=VMEM_BYTES),
        cost_estimate=pl.CostEstimate(
            flops=heads * length * length * 256 * 10,
            bytes_accessed=heads * length * length * 4,
            transcendentals=0,
        ),
        name="attend_back",
    )(q, k, v, d_ctx, ctx, probs)


def swap(values, bit):
    return lax.ppermute(values, "shard", [(i, i ^ bit) for i in range(8)])


def place_kernel(*refs):
    *pieces, whole, sems = refs
    me = lax.axis_index("shard")
    rows = pieces[0].shape[0]
    half = rows // 2
    copies = []
    for core in (0, 1):
        own, over_x, over_y, top, bottom = pieces[core * 5 : core * 5 + 5]
        for piece, bits, shift in (
            (own, 0, 0),
            (over_x, 2, 0),
            (over_y, 4, 0),
            (top, 6, 0),
            (bottom, 6, half),
        ):
            owner = flip(me, bits + core)
            start = pl.multiple_of(owner * rows + shift, 16)
            copies.append(
                pltpu.make_async_copy(
                    piece, whole.at[pl.ds(start, piece.shape[0])], sems.at[len(copies)]
                )
            )
    for copy in copies:
        copy.start()
    for copy in copies:
        copy.wait()


def flip(index, bits):
    result = index
    for bit in (1, 2, 4):
        if bits & bit:
            held = lax.rem(index // bit, 2)
            result = result + bit - 2 * bit * held
    return result


def gather_shard(piece):
    rows, columns = piece.shape
    half = rows // 2
    over_x = swap(piece, 2)
    over_y = swap(piece, 4)
    top = swap(over_x[:half], 4)
    bottom = swap(over_y[half:], 2)
    near = [piece, over_x, over_y, top, bottom]
    far = [swap(part, 1) for part in near]
    return pl.pallas_call(
        place_kernel,
        in_specs=[pl.BlockSpec(memory_space=pl.ANY)] * 10,
        out_specs=pl.BlockSpec(memory_space=pltpu.VMEM),
        compiler_params=pltpu.CompilerParams(vmem_limit_bytes=VMEM_BYTES),
        out_shape=jax.ShapeDtypeStruct((8 * rows, columns), piece.dtype),
        scratch_shapes=[pltpu.SemaphoreType.DMA((10,))],
        cost_estimate=pl.CostEstimate(
            flops=0, bytes_accessed=32 * rows * columns, transcendentals=0
        ),
        name="place_rows",
    )(*near, *far)


def add_low(a, b):
    return (a.astype(jnp.float32) + b.astype(jnp.float32)).astype(jnp.bfloat16)


def pick(values, index, axis):
    return lax.dynamic_index_in_dim(values, index, axis, keepdims=False)


def scatter_shard(whole):
    me = lax.axis_index("shard")
    core, x, y = me % 2, (me // 2) % 2, me // 4
    _, rows, columns = whole.shape
    half = rows // 32 * 16
    parts = whole.reshape(4, 2, rows, columns)
    mine = add_low(pick(parts, core, 1), swap(pick(parts, 1 - core, 1), 1))
    mine = mine.reshape(2, 2, rows, columns)
    left, right = mine[:, :, :half], mine[:, :, half:]
    left = add_low(pick(left, x, 1), swap(pick(left, 1 - x, 1), 2))
    right = add_low(pick(right, y, 0), swap(pick(right, 1 - y, 0), 4))
    left = add_low(pick(left, y, 0), swap(pick(left, 1 - y, 0), 4))
    right = add_low(pick(right, x, 0), swap(pick(right, 1 - x, 0), 2))
    return jnp.concatenate([left, right], axis=0)


def share_vector(vector):
    rows = jnp.zeros((8, vector.shape[0]), vector.dtype)
    rows = lax.dynamic_update_slice_in_dim(rows, vector[None], lax.axis_index("shard"), 0)
    for bit in (1, 2, 4):
        rows = rows + swap(rows, bit)
    return rows


def gather_ctx(piece):
    copies = jnp.broadcast_to(piece[None], (lax.axis_size("ctx"), *piece.shape))
    return lax.all_to_all(copies, "ctx", 0, 0, tiled=True)


def extra_rows(first, second, columns):
    rows = [jnp.pad(part, ((0, 0), (0, columns - part.shape[1]))) for part in (first, second)]
    return jnp.pad(jnp.stack(rows, axis=1), ((0, 0), (0, 14), (0, 0))).astype(jnp.bfloat16)


def local_fast(
    tokens,
    cotangent,
    doc_lengths,
    w_qkv,
    w_out,
    w_in,
    w_down,
    bias_query,
    bias_value,
    bias_out,
    gain_attn,
    shift_attn,
    bias_in,
    bias_down,
    gain_ffn,
    shift_ffn,
):
    blocks = lax.axis_size("ctx")
    place = lax.axis_index("ctx")
    inputs = tokens[0]
    rows, width = inputs.shape
    length = rows * blocks
    share = width // blocks
    vectors = [
        bias_query,
        bias_value,
        bias_out,
        gain_attn,
        shift_attn,
        bias_in,
        bias_down,
        gain_ffn,
        shift_ffn,
    ]
    sizes = [vector.shape[0] for vector in vectors]

    tokens_all = gather_ctx(inputs).reshape(length, width)
    qkv_part = lax.dynamic_index_in_dim(
        w_qkv.reshape(w_qkv.shape[0], 3, blocks, share), place, 2, keepdims=False
    ).reshape(w_qkv.shape[0], 3 * share)
    mat_qkv = gather_shard(qkv_part)
    packed = share_vector(jnp.concatenate(vectors))
    mat_out = gather_shard(w_out)
    mat_in = gather_shard(w_in)
    mat_down = gather_shard(w_down)
    edges = [sum(sizes[:i]) for i in range(len(sizes) + 1)]
    vec_query, vec_value, vec_out, gain_a, shift_a, vec_in, vec_down, gain_f, shift_f = [
        packed[:, edges[i] : edges[i + 1]].reshape(-1).astype(jnp.float32)
        for i in range(len(sizes))
    ]

    ids = segment_ids(doc_lengths[0], length)
    bias_q = lax.dynamic_slice_in_dim(vec_query, place * share, share)
    bias_v = lax.dynamic_slice_in_dim(vec_value, place * share, share)
    proj = lax.dot_general(
        mat_qkv, tokens_all, (((0,), (1,)), ((), ())), preferred_element_type=jnp.float32
    )
    query = (proj[:share] + bias_q[:, None]).astype(jnp.bfloat16)
    key = proj[share : 2 * share].astype(jnp.bfloat16)
    value = (proj[2 * share :] + bias_v[:, None]).astype(jnp.bfloat16)
    mixed, probs = attend(ids, query, key, value)
    context = lax.all_to_all(mixed, "ctx", 1, 0, tiled=True)

    resid_attn = inputs.astype(jnp.float32) + (dot(context, mat_out, TN) + vec_out)
    hidden = layer_norm(resid_attn, gain_a, shift_a)
    hidden_low = hidden.astype(jnp.bfloat16)
    gate = dot(hidden_low, mat_in) + vec_in
    active = gelu_exact(gate).astype(jnp.bfloat16)
    resid_ffn = hidden + (dot(active, mat_down) + vec_down)
    layer_out = layer_norm(resid_ffn, gain_f, shift_f).astype(jnp.bfloat16)

    upstream = cotangent[0].astype(jnp.float32)
    _, norm_ffn_back = jax.vjp(layer_norm, resid_ffn, gain_f, shift_f)
    grad_resid_ffn, g_gain_f, g_shift_f = norm_ffn_back(upstream)
    d_ffn = grad_resid_ffn.astype(jnp.bfloat16)
    g_down = dot(active, d_ffn, TN).astype(jnp.bfloat16)
    g_bdown = column_sums(d_ffn)
    d_ffn, g_down = lax.optimization_barrier((d_ffn, g_down))
    s_down = scatter_shard(g_down.reshape(8, -1, width))
    d_active = dot(d_ffn, mat_down, NT)
    _, gelu_back = jax.vjp(gelu_exact, gate)
    d_gate = gelu_back(d_active)[0].astype(jnp.bfloat16)
    g_in = dot(hidden_low, d_gate, TN).astype(jnp.bfloat16)
    g_bin = column_sums(d_gate)
    d_gate, g_in = lax.optimization_barrier((d_gate, g_in))
    s_in = scatter_shard(g_in.reshape(8, width // 8, -1))
    d_hidden = grad_resid_ffn + dot(d_gate, mat_in, NT)
    _, norm_attn_back = jax.vjp(layer_norm, resid_attn, gain_a, shift_a)
    grad_resid_attn, g_gain_a, g_shift_a = norm_attn_back(d_hidden)
    d_attn = grad_resid_attn.astype(jnp.bfloat16)
    g_out = dot(context, d_attn).astype(jnp.bfloat16)
    g_bout = column_sums(d_attn)
    d_context = dot(mat_out, d_attn, NT).astype(jnp.bfloat16)

    d_mixed = lax.all_to_all(d_context, "ctx", 0, 1, tiled=True)
    small = [g_bout, g_gain_a, g_shift_a, g_bin, g_bdown, g_gain_f, g_shift_f]
    small = jnp.concatenate([part.reshape(8, -1) for part in small], axis=1)
    own = width // 8
    g_out = jnp.concatenate(
        [g_out.reshape(8, own, width), extra_rows(small[:, :width], small[:, width:], width)],
        axis=1,
    )
    s_out = scatter_shard(g_out)
    d_query, d_key, d_value = attend_back(query, key, value, d_mixed, mixed, probs)
    d_proj = jnp.concatenate([d_query, d_key, d_value], axis=0)
    g_qkv = lax.dot_general(
        tokens_all, d_proj, (((0,), (1,)), ((), ())), preferred_element_type=jnp.float32
    ).astype(jnp.bfloat16)
    columns = 3 * share
    sums = [
        jnp.sum(part.astype(jnp.float32), axis=1).reshape(-1, own) for part in (d_query, d_value)
    ]
    first = place * (share // own)
    sums = [
        lax.dynamic_update_slice_in_dim(jnp.zeros((8, own), jnp.float32), part, first, 0)
        for part in sums
    ]
    g_qkv = jnp.concatenate(
        [g_qkv.reshape(8, own, columns), extra_rows(sums[0], sums[1], columns)], axis=1
    )
    s_qkv = scatter_shard(g_qkv)
    spread = dot(d_proj, mat_qkv, (((0,), (1,)), ((), ()))).astype(jnp.bfloat16)
    spread = lax.all_to_all(spread.reshape(blocks, rows, width), "ctx", 0, 0, tiled=True)
    grad_tokens = grad_resid_attn + jnp.sum(spread.astype(jnp.float32), axis=0)
    all_qkv = gather_ctx(s_qkv)
    out_qkv = all_qkv[:, :own].reshape(blocks, own, 3, share).transpose(1, 2, 0, 3)
    out_qkv = out_qkv.reshape(own, 3 * width).astype(jnp.float32)
    out_query, out_value = [
        jnp.sum(all_qkv[:, own + i, :own].astype(jnp.float32), axis=0) for i in (0, 1)
    ]
    out_down, out_in, out_out = [
        part.astype(jnp.float32) for part in lax.psum((s_down, s_in, s_out), "ctx")
    ]
    small = jnp.concatenate([out_out[own], out_out[own + 1]])
    ends = [edge - edges[2] for edge in edges[2:]]
    small = [small[ends[i] : ends[i + 1]] for i in range(len(ends) - 1)]
    out_out = out_out[:own]
    return (
        layer_out[None],
        grad_tokens[None],
        out_qkv,
        out_out,
        out_in,
        out_down,
        out_query,
        out_value,
        *small,
    )


def solution(mesh):
    sizes = (mesh.shape["shard"], mesh.shape["ctx"])
    chosen = local_fast if sizes == (8, 4) else local_any
    return jax.shard_map(
        chosen,
        mesh=mesh,
        in_specs=(
            P("shard", "ctx", None),
            P("shard", "ctx", None),
            P("shard", None),
            P("shard", None),
            P("shard", None),
            P("shard", None),
            P("shard", None),
            P("shard"),
            P("shard"),
            P("shard"),
            P("shard"),
            P("shard"),
            P("shard"),
            P("shard"),
            P("shard"),
            P("shard"),
        ),
        out_specs=(
            P("shard", "ctx", None),
            P("shard", "ctx", None),
            P("shard", None),
            P("shard", None),
            P("shard", None),
            P("shard", None),
            P("shard"),
            P("shard"),
            P("shard"),
            P("shard"),
            P("shard"),
            P("shard"),
            P("shard"),
            P("shard"),
            P("shard"),
        ),
        check_vma=False,
    )
```

```python
import functools

import jax
import jax.numpy as jnp
from jax import lax
from jax.experimental import pallas as pl
from jax.experimental.pallas import tpu as pltpu
from jax.sharding import PartitionSpec as P

HEADS = 12
HEAD = 64


epsilon = 1e-12
scale_attn = 0.125


def layer_norm(values, gain, shift):
    center = values - jnp.mean(values, axis=-1, keepdims=True)
    spread = jnp.mean(center * center, axis=-1, keepdims=True)
    return center * lax.rsqrt(spread + epsilon) * gain + shift


def gelu_exact(values):
    return jax.nn.gelu(values, approximate=False)


def segment_ids(counts, length):
    places = jnp.arange(length, dtype=jnp.int32)
    first_end = counts[0]
    second_end = first_end + counts[1]
    third_end = second_end + counts[2]
    return (
        (places >= first_end).astype(jnp.int32)
        + (places >= second_end).astype(jnp.int32)
        + (places >= third_end).astype(jnp.int32)
    )


def split_heads(values):
    return values.reshape(values.shape[0], HEADS, HEAD).transpose(1, 0, 2)


def join_heads(values):
    return values.transpose(1, 0, 2).reshape(values.shape[1], HEADS * HEAD)


def head_forward(query_h, key_h, value_h, match_mask):
    scores = (
        jnp.einsum("qd,kd->qk", query_h, key_h, preferred_element_type=jnp.float32) * scale_attn
    )
    scores = jnp.where(match_mask, scores, -1000000000.0)
    maximum = jnp.max(scores, axis=-1, keepdims=True)
    exp_terms = jnp.exp(scores - maximum)
    total = jnp.sum(exp_terms, axis=-1, keepdims=True)
    weights_soft = (exp_terms / total).astype(jnp.bfloat16)
    mixed = jnp.dot(weights_soft, value_h, preferred_element_type=jnp.float32)
    return (mixed, (maximum + jnp.log(total))[:, 0])


def head_backward(query_h, key_h, value_h, dctx_h, log_total, match_mask):
    scores = (
        jnp.einsum("qd,kd->qk", query_h, key_h, preferred_element_type=jnp.float32) * scale_attn
    )
    probs = jnp.where(match_mask, jnp.exp(scores - log_total[:, None]), 0.0)
    grad_probs = jnp.einsum("qd,kd->qk", dctx_h, value_h, preferred_element_type=jnp.float32)
    grad_value = jnp.einsum(
        "qk,qd->kd", probs.astype(jnp.bfloat16), dctx_h, preferred_element_type=jnp.float32
    )
    inner = jnp.sum(probs * grad_probs, axis=-1, keepdims=True)
    grad_scores = (probs * (grad_probs - inner) * scale_attn).astype(jnp.bfloat16)
    grad_query = jnp.dot(grad_scores, key_h, preferred_element_type=jnp.float32)
    grad_key = jnp.einsum("qk,qd->kd", grad_scores, query_h, preferred_element_type=jnp.float32)
    return (grad_query, grad_key, grad_value)


def column_sums(values):
    return jnp.sum(values.astype(jnp.float32), axis=0)


def local_any(
    tokens,
    cotangent,
    doc_lengths,
    w_qkv,
    w_out,
    w_in,
    w_down,
    bias_query,
    bias_value,
    bias_out,
    gain_attn,
    shift_attn,
    bias_in,
    bias_down,
    gain_ffn,
    shift_ffn,
):
    gathered = (
        lax.all_gather(w_qkv, "shard", axis=0, tiled=True),
        lax.all_gather(w_out, "shard", axis=0, tiled=True),
        lax.all_gather(w_in, "shard", axis=0, tiled=True),
        lax.all_gather(w_down, "shard", axis=0, tiled=True),
        lax.all_gather(bias_query, "shard", axis=0, tiled=True),
        lax.all_gather(bias_value, "shard", axis=0, tiled=True),
        lax.all_gather(bias_out, "shard", axis=0, tiled=True),
        lax.all_gather(gain_attn, "shard", axis=0, tiled=True),
        lax.all_gather(shift_attn, "shard", axis=0, tiled=True),
        lax.all_gather(bias_in, "shard", axis=0, tiled=True),
        lax.all_gather(bias_down, "shard", axis=0, tiled=True),
        lax.all_gather(gain_ffn, "shard", axis=0, tiled=True),
        lax.all_gather(shift_ffn, "shard", axis=0, tiled=True),
    )
    mat_qkv, mat_out, mat_in, mat_down = (gathered[0], gathered[1], gathered[2], gathered[3])
    vec_query, vec_value, vec_out, gain_a, shift_a, vec_in, vec_down, gain_f, shift_f = [
        piece.astype(jnp.float32) for piece in gathered[4:]
    ]
    rows = tokens.shape[1]
    width = tokens.shape[2]
    inputs = tokens[0]
    length = rows * lax.axis_size("ctx")
    all_ids = segment_ids(doc_lengths[0], length)
    own_ids = lax.dynamic_slice_in_dim(all_ids, lax.axis_index("ctx") * rows, rows)
    match_mask = own_ids[:, None] == all_ids[None, :]
    projected = jnp.dot(inputs, mat_qkv, preferred_element_type=jnp.float32)
    query = (projected[:, :width] + vec_query).astype(jnp.bfloat16)
    key_local = projected[:, width : 2 * width].astype(jnp.bfloat16)
    value_local = (projected[:, 2 * width :] + vec_value).astype(jnp.bfloat16)
    key_all, value_all = (
        lax.all_gather(key_local, "ctx", axis=0, tiled=True),
        lax.all_gather(value_local, "ctx", axis=0, tiled=True),
    )
    query_heads = split_heads(query)
    key_heads = split_heads(key_all)
    value_heads = split_heads(value_all)
    mixed, log_total = lax.map(
        lambda items: head_forward(items[0], items[1], items[2], match_mask),
        (query_heads, key_heads, value_heads),
    )
    context = join_heads(mixed).astype(jnp.bfloat16)
    resid_attn = inputs.astype(jnp.float32) + (
        jnp.dot(context, mat_out, preferred_element_type=jnp.float32) + vec_out
    )
    hidden = layer_norm(resid_attn, gain_a, shift_a)
    hidden_low = hidden.astype(jnp.bfloat16)
    gate = jnp.dot(hidden_low, mat_in, preferred_element_type=jnp.float32) + vec_in
    active = gelu_exact(gate).astype(jnp.bfloat16)
    resid_ffn = hidden + (jnp.dot(active, mat_down, preferred_element_type=jnp.float32) + vec_down)
    layer_out = layer_norm(resid_ffn, gain_f, shift_f).astype(jnp.bfloat16)
    regathered = (
        lax.all_gather(w_qkv, "shard", axis=0, tiled=True),
        lax.all_gather(w_out, "shard", axis=0, tiled=True),
        lax.all_gather(w_in, "shard", axis=0, tiled=True),
        lax.all_gather(w_down, "shard", axis=0, tiled=True),
    )
    mat_qkv, mat_out, mat_in, mat_down = (
        regathered[0],
        regathered[1],
        regathered[2],
        regathered[3],
    )
    upstream = cotangent[0].astype(jnp.float32)
    _, norm_ffn_back = jax.vjp(layer_norm, resid_ffn, gain_f, shift_f)
    grad_resid_ffn, g_gain_f, g_shift_f = norm_ffn_back(upstream)
    d_ffn = grad_resid_ffn.astype(jnp.bfloat16)
    g_down = jnp.einsum("tf,td->fd", active, d_ffn, preferred_element_type=jnp.float32)
    g_bdown = column_sums(d_ffn)
    d_active = jnp.einsum("td,fd->tf", d_ffn, mat_down, preferred_element_type=jnp.float32)
    _, gelu_back = jax.vjp(gelu_exact, gate)
    d_gate = gelu_back(d_active)[0].astype(jnp.bfloat16)
    g_in = jnp.einsum("td,tf->df", hidden_low, d_gate, preferred_element_type=jnp.float32)
    g_bin = column_sums(d_gate)
    d_hidden = grad_resid_ffn + jnp.einsum(
        "tf,df->td", d_gate, mat_in, preferred_element_type=jnp.float32
    )
    _, norm_attn_back = jax.vjp(layer_norm, resid_attn, gain_a, shift_a)
    grad_resid_attn, g_gain_a, g_shift_a = norm_attn_back(d_hidden)
    d_attn = grad_resid_attn.astype(jnp.bfloat16)
    g_out = jnp.einsum("tc,td->cd", context, d_attn, preferred_element_type=jnp.float32)
    g_bout = column_sums(d_attn)
    d_context = jnp.einsum("td,cd->tc", d_attn, mat_out, preferred_element_type=jnp.float32).astype(
        jnp.bfloat16
    )
    dctx_heads = split_heads(d_context)
    grad_query, grad_key, grad_value = lax.map(
        lambda items: head_backward(items[0], items[1], items[2], items[3], items[4], match_mask),
        (query_heads, key_heads, value_heads, dctx_heads, log_total),
    )
    key_terms = join_heads(grad_key)
    value_terms = join_heads(grad_value)
    key_summed, value_summed = (
        lax.psum_scatter(
            key_terms.astype(jnp.bfloat16), "ctx", scatter_dimension=0, tiled=True
        ).astype(jnp.float32),
        lax.psum_scatter(
            value_terms.astype(jnp.bfloat16), "ctx", scatter_dimension=0, tiled=True
        ).astype(jnp.float32),
    )
    d_query = join_heads(grad_query).astype(jnp.bfloat16)
    d_key = key_summed.astype(jnp.bfloat16)
    d_value = value_summed.astype(jnp.bfloat16)
    d_proj = jnp.concatenate([d_query, d_key, d_value], axis=1)
    g_qkv = jnp.einsum("td,te->de", inputs, d_proj, preferred_element_type=jnp.float32)
    g_query = column_sums(d_query)
    g_value = column_sums(d_value)
    grad_tokens = grad_resid_attn + jnp.einsum(
        "te,de->td", d_proj, mat_qkv, preferred_element_type=jnp.float32
    )
    group_parts = (
        lax.psum_scatter(
            g_qkv.astype(jnp.bfloat16), "shard", scatter_dimension=0, tiled=True
        ).astype(jnp.float32),
        lax.psum_scatter(
            g_out.astype(jnp.bfloat16), "shard", scatter_dimension=0, tiled=True
        ).astype(jnp.float32),
        lax.psum_scatter(
            g_in.astype(jnp.bfloat16), "shard", scatter_dimension=0, tiled=True
        ).astype(jnp.float32),
        lax.psum_scatter(
            g_down.astype(jnp.bfloat16), "shard", scatter_dimension=0, tiled=True
        ).astype(jnp.float32),
        lax.psum_scatter(
            g_query.astype(jnp.bfloat16), "shard", scatter_dimension=0, tiled=True
        ).astype(jnp.float32),
        lax.psum_scatter(
            g_value.astype(jnp.bfloat16), "shard", scatter_dimension=0, tiled=True
        ).astype(jnp.float32),
        lax.psum_scatter(
            g_bout.astype(jnp.bfloat16), "shard", scatter_dimension=0, tiled=True
        ).astype(jnp.float32),
        lax.psum_scatter(
            g_gain_a.astype(jnp.bfloat16), "shard", scatter_dimension=0, tiled=True
        ).astype(jnp.float32),
        lax.psum_scatter(
            g_shift_a.astype(jnp.bfloat16), "shard", scatter_dimension=0, tiled=True
        ).astype(jnp.float32),
        lax.psum_scatter(
            g_bin.astype(jnp.bfloat16), "shard", scatter_dimension=0, tiled=True
        ).astype(jnp.float32),
        lax.psum_scatter(
            g_bdown.astype(jnp.bfloat16), "shard", scatter_dimension=0, tiled=True
        ).astype(jnp.float32),
        lax.psum_scatter(
            g_gain_f.astype(jnp.bfloat16), "shard", scatter_dimension=0, tiled=True
        ).astype(jnp.float32),
        lax.psum_scatter(
            g_shift_f.astype(jnp.bfloat16), "shard", scatter_dimension=0, tiled=True
        ).astype(jnp.float32),
    )
    (
        p_qkv,
        p_out,
        p_in,
        p_down,
        p_query,
        p_value,
        p_bout,
        p_gain_a,
        p_shift_a,
        p_bin,
        p_bdown,
        p_gain_f,
        p_shift_f,
    ) = group_parts
    summed = (
        lax.psum(p_qkv.astype(jnp.bfloat16), "ctx").astype(jnp.float32),
        lax.psum(p_out.astype(jnp.bfloat16), "ctx").astype(jnp.float32),
        lax.psum(p_in.astype(jnp.bfloat16), "ctx").astype(jnp.float32),
        lax.psum(p_down.astype(jnp.bfloat16), "ctx").astype(jnp.float32),
        lax.psum(p_query.astype(jnp.bfloat16), "ctx").astype(jnp.float32),
        lax.psum(p_value.astype(jnp.bfloat16), "ctx").astype(jnp.float32),
        lax.psum(p_bout.astype(jnp.bfloat16), "ctx").astype(jnp.float32),
        lax.psum(p_gain_a.astype(jnp.bfloat16), "ctx").astype(jnp.float32),
        lax.psum(p_shift_a.astype(jnp.bfloat16), "ctx").astype(jnp.float32),
        lax.psum(p_bin.astype(jnp.bfloat16), "ctx").astype(jnp.float32),
        lax.psum(p_bdown.astype(jnp.bfloat16), "ctx").astype(jnp.float32),
        lax.psum(p_gain_f.astype(jnp.bfloat16), "ctx").astype(jnp.float32),
        lax.psum(p_shift_f.astype(jnp.bfloat16), "ctx").astype(jnp.float32),
    )
    return (
        layer_out[None],
        grad_tokens[None],
        summed[0],
        summed[1],
        summed[2],
        summed[3],
        summed[4],
        summed[5],
        summed[6],
        summed[7],
        summed[8],
        summed[9],
        summed[10],
        summed[11],
        summed[12],
    )


QUERY_BLOCK = 256
VMEM_BYTES = 56 * 1024 * 1024
TN = (((0,), (0,)), ((), ()))
NT = (((1,), (1,)), ((), ()))


def dot(a, b, dims=(((1,), (0,)), ((), ()))):
    return lax.dot_general(a, b, dims, preferred_element_type=jnp.float32)


def attend_kernel(ids_row, ids_col, q_ref, k_ref, v_ref, ctx_ref, p_ref):
    scores = dot(k_ref[...], q_ref[...] * jnp.bfloat16(0.125), TN)
    scores = jnp.where(ids_col[...] == ids_row[...], scores, -1000000000.0)
    maximum = jnp.max(scores, axis=0, keepdims=True)
    terms = jnp.exp(scores - maximum)
    total = jnp.sum(terms, axis=0, keepdims=True)
    probs = (terms * (1.0 / total)).astype(jnp.bfloat16)
    p_ref[0] = probs
    ctx_ref[...] = dot(v_ref[...], probs).astype(jnp.bfloat16)


def attend(ids, q, k, v):
    width, length = q.shape
    heads = width // HEAD
    block = QUERY_BLOCK
    row = pl.BlockSpec((HEAD, length), lambda h, b: (h, 0))
    part = pl.BlockSpec((HEAD, block), lambda h, b: (h, b))
    return pl.pallas_call(
        attend_kernel,
        grid=(heads, length // block),
        in_specs=[
            pl.BlockSpec((1, block), lambda h, b: (0, b)),
            pl.BlockSpec((length, 1), lambda h, b: (0, 0)),
            part,
            row,
            row,
        ],
        out_specs=[part, pl.BlockSpec((1, length, block), lambda h, b: (h, 0, b))],
        out_shape=[
            jax.ShapeDtypeStruct((width, length), jnp.bfloat16),
            jax.ShapeDtypeStruct((heads, length, length), jnp.bfloat16),
        ],
        compiler_params=pltpu.CompilerParams(vmem_limit_bytes=VMEM_BYTES),
        cost_estimate=pl.CostEstimate(
            flops=heads * length * length * 256 * 4,
            bytes_accessed=heads * length * length * 4,
            transcendentals=heads * length * length,
        ),
        name="attend",
    )(ids[None, :], ids[:, None], q, k, v)


def attend_back_kernel(
    q_ref, k_ref, v_ref, d_ref, ctx_ref, p_ref, dq_ref, dk_ref, dv_ref, dk_sum, dv_sum
):
    step = pl.program_id(1)

    @pl.when(step == 0)
    def _():
        dk_sum[...] = jnp.zeros_like(dk_sum)
        dv_sum[...] = jnp.zeros_like(dv_sum)

    probs = p_ref[0]
    d_ctx = d_ref[...]
    inner = jnp.sum(
        d_ctx.astype(jnp.float32) * ctx_ref[...].astype(jnp.float32), axis=0, keepdims=True
    )
    d_probs = dot(v_ref[...], d_ctx, TN)
    d_scores = (probs.astype(jnp.float32) * (d_probs - inner)).astype(jnp.bfloat16)
    dq_ref[...] = (dot(k_ref[...], d_scores) * 0.125).astype(jnp.bfloat16)
    dk_sum[...] += dot(d_scores, q_ref[...], NT)
    dv_sum[...] += dot(probs, d_ctx, NT)

    @pl.when(step == pl.num_programs(1) - 1)
    def _():
        dk_ref[...] = (dk_sum[...].T * 0.125).astype(jnp.bfloat16)
        dv_ref[...] = dv_sum[...].T.astype(jnp.bfloat16)


def attend_back(q, k, v, d_ctx, ctx, probs, first):
    width, length = q.shape
    heads = width // HEAD
    block = QUERY_BLOCK
    row = pl.BlockSpec((HEAD, length), lambda h, b: (h, 0))
    part = pl.BlockSpec((HEAD, block), lambda h, b: (h, b))
    shape = jax.ShapeDtypeStruct((width, length), jnp.bfloat16)
    return pl.pallas_call(
        attend_back_kernel,
        grid=(heads, length // block),
        in_specs=[
            part,
            row,
            row,
            part,
            part,
            pl.BlockSpec((1, length, block), lambda h, b: (first + h, 0, b)),
        ],
        out_specs=[part, row, row],
        out_shape=[shape, shape, shape],
        scratch_shapes=[pltpu.VMEM((length, HEAD), jnp.float32)] * 2,
        compiler_params=pltpu.CompilerParams(vmem_limit_bytes=VMEM_BYTES),
        cost_estimate=pl.CostEstimate(
            flops=heads * length * length * 256 * 10,
            bytes_accessed=heads * length * length * 4,
            transcendentals=0,
        ),
        name="attend_back",
    )(q, k, v, d_ctx, ctx, probs)


def swap(values, bit):
    return lax.ppermute(values, "shard", [(i, i ^ bit) for i in range(8)])


def place_kernel(*refs):
    *pieces, whole, sems = refs
    me = lax.axis_index("shard")
    rows = pieces[0].shape[0]
    half = rows // 2
    copies = []
    for core in (0, 1):
        own, over_x, over_y, top, bottom = pieces[core * 5 : core * 5 + 5]
        for piece, bits, shift in (
            (own, 0, 0),
            (over_x, 2, 0),
            (over_y, 4, 0),
            (top, 6, 0),
            (bottom, 6, half),
        ):
            owner = flip(me, bits + core)
            start = pl.multiple_of(owner * rows + shift, 16)
            copies.append(
                pltpu.make_async_copy(
                    piece, whole.at[pl.ds(start, piece.shape[0])], sems.at[len(copies)]
                )
            )
    for copy in copies:
        copy.start()
    for copy in copies:
        copy.wait()


def flip(index, bits):
    result = index
    for bit in (1, 2, 4):
        if bits & bit:
            held = lax.rem(index // bit, 2)
            result = result + bit - 2 * bit * held
    return result


def gather_shard(piece):
    rows, columns = piece.shape
    half = rows // 2
    over_x = swap(piece, 2)
    over_y = swap(piece, 4)
    top = swap(over_x[:half], 4)
    bottom = swap(over_y[half:], 2)
    near = [piece, over_x, over_y, top, bottom]
    far = [swap(part, 1) for part in near]
    return pl.pallas_call(
        place_kernel,
        in_specs=[pl.BlockSpec(memory_space=pl.ANY)] * 10,
        out_specs=pl.BlockSpec(memory_space=pltpu.VMEM),
        compiler_params=pltpu.CompilerParams(vmem_limit_bytes=VMEM_BYTES),
        out_shape=jax.ShapeDtypeStruct((8 * rows, columns), piece.dtype),
        scratch_shapes=[pltpu.SemaphoreType.DMA((10,))],
        cost_estimate=pl.CostEstimate(
            flops=0, bytes_accessed=32 * rows * columns, transcendentals=0
        ),
        name="place_rows",
    )(*near, *far)


def add_low(a, b):
    return (a.astype(jnp.float32) + b.astype(jnp.float32)).astype(jnp.bfloat16)


def pick(values, index, axis):
    return lax.dynamic_index_in_dim(values, index, axis, keepdims=False)


def halve_core(whole):
    core = lax.axis_index("shard") % 2
    _, rows, columns = whole.shape
    parts = whole.reshape(4, 2, rows, columns)
    mine = add_low(pick(parts, core, 1), swap(pick(parts, 1 - core, 1), 1))
    return mine.reshape(2, 2, rows, columns)


def halve_first(mine):
    me = lax.axis_index("shard")
    x, y = (me // 2) % 2, me // 4
    half = mine.shape[2] // 32 * 16
    upper, lower = mine[:, :, :half], mine[:, :, half:]
    upper = add_low(pick(upper, x, 1), swap(pick(upper, 1 - x, 1), 2))
    lower = add_low(pick(lower, y, 0), swap(pick(lower, 1 - y, 0), 4))
    return upper, lower


def halve_second(pair):
    me = lax.axis_index("shard")
    x, y = (me // 2) % 2, me // 4
    upper, lower = pair
    upper = add_low(pick(upper, y, 0), swap(pick(upper, 1 - y, 0), 4))
    lower = add_low(pick(lower, x, 0), swap(pick(lower, 1 - x, 0), 2))
    return jnp.concatenate([upper, lower], axis=0)


def sum_shares(piece, axis):
    blocks = lax.axis_size("ctx")
    parts = lax.all_to_all(piece, "ctx", axis, 0, tiled=True)
    parts = parts.reshape(blocks, -1, parts.shape[1])
    return jnp.sum(parts.astype(jnp.float32), axis=0).astype(jnp.bfloat16)


def gather_line(piece):
    blocks, place = lax.axis_size("ctx"), lax.axis_index("ctx")
    up = [(i, i + 1) for i in range(blocks - 1)]
    down = [(i + 1, i) for i in range(blocks - 1)]
    from_below, from_above = [piece], [piece]
    for _ in range(blocks - 1):
        from_below.append(lax.ppermute(from_below[-1], "ctx", up))
        from_above.append(lax.ppermute(from_above[-1], "ctx", down))
    whole = jnp.zeros((blocks, *piece.shape), piece.dtype)
    whole = lax.dynamic_update_index_in_dim(whole, piece, place, 0)
    for d in range(1, blocks):
        block = from_below[d] + from_above[blocks - d]
        whole = lax.dynamic_update_index_in_dim(whole, block, (place - d) % blocks, 0)
    return whole


def share_vector(vector):
    rows = jnp.zeros((8, vector.shape[0]), vector.dtype)
    rows = lax.dynamic_update_slice_in_dim(rows, vector[None], lax.axis_index("shard"), 0)
    for bit in (1, 2, 4):
        rows = rows + swap(rows, bit)
    return rows


def gather_ctx(piece):
    copies = jnp.broadcast_to(piece[None], (lax.axis_size("ctx"), *piece.shape))
    return lax.all_to_all(copies, "ctx", 0, 0, tiled=True)


def extra_rows(first, second, columns):
    rows = [jnp.pad(part, ((0, 0), (0, columns - part.shape[1]))) for part in (first, second)]
    return jnp.pad(jnp.stack(rows, axis=1), ((0, 0), (0, 14), (0, 0))).astype(jnp.bfloat16)


def local_fast(
    tokens,
    cotangent,
    doc_lengths,
    w_qkv,
    w_out,
    w_in,
    w_down,
    bias_query,
    bias_value,
    bias_out,
    gain_attn,
    shift_attn,
    bias_in,
    bias_down,
    gain_ffn,
    shift_ffn,
):
    blocks = lax.axis_size("ctx")
    place = lax.axis_index("ctx")
    inputs = tokens[0]
    rows, width = inputs.shape
    length = rows * blocks
    share = width // blocks
    vectors = [
        bias_query,
        bias_value,
        bias_out,
        gain_attn,
        shift_attn,
        bias_in,
        bias_down,
        gain_ffn,
        shift_ffn,
    ]
    sizes = [vector.shape[0] for vector in vectors]

    tokens_all = gather_line(inputs).reshape(length, width)
    qkv_part = lax.dynamic_index_in_dim(
        w_qkv.reshape(w_qkv.shape[0], 3, blocks, share), place, 2, keepdims=False
    ).reshape(w_qkv.shape[0], 3 * share)
    mat_qkv = gather_shard(qkv_part)
    packed = share_vector(jnp.concatenate(vectors))
    mat_out = gather_shard(w_out)
    mat_in = gather_shard(w_in)
    mat_down = gather_shard(w_down)
    edges = [sum(sizes[:i]) for i in range(len(sizes) + 1)]
    vec_query, vec_value, vec_out, gain_a, shift_a, vec_in, vec_down, gain_f, shift_f = [
        packed[:, edges[i] : edges[i + 1]].reshape(-1).astype(jnp.float32)
        for i in range(len(sizes))
    ]

    ids = segment_ids(doc_lengths[0], length)
    bias_q = lax.dynamic_slice_in_dim(vec_query, place * share, share)
    bias_v = lax.dynamic_slice_in_dim(vec_value, place * share, share)
    proj = lax.dot_general(
        mat_qkv, tokens_all, (((0,), (1,)), ((), ())), preferred_element_type=jnp.float32
    )
    query = (proj[:share] + bias_q[:, None]).astype(jnp.bfloat16)
    key = proj[share : 2 * share].astype(jnp.bfloat16)
    value = (proj[2 * share :] + bias_v[:, None]).astype(jnp.bfloat16)
    mixed, probs = attend(ids, query, key, value)
    context = lax.all_to_all(mixed, "ctx", 1, 0, tiled=True)

    resid_attn = inputs.astype(jnp.float32) + (dot(context, mat_out, TN) + vec_out)
    hidden = layer_norm(resid_attn, gain_a, shift_a)
    hidden_low = hidden.astype(jnp.bfloat16)
    gate = dot(hidden_low, mat_in) + vec_in
    active = gelu_exact(gate).astype(jnp.bfloat16)
    resid_ffn = hidden + (dot(active, mat_down) + vec_down)
    layer_out = layer_norm(resid_ffn, gain_f, shift_f).astype(jnp.bfloat16)

    upstream = cotangent[0].astype(jnp.float32)
    _, norm_ffn_back = jax.vjp(layer_norm, resid_ffn, gain_f, shift_f)
    grad_resid_ffn, g_gain_f, g_shift_f = norm_ffn_back(upstream)
    d_ffn = grad_resid_ffn.astype(jnp.bfloat16)
    g_down = dot(active, d_ffn, TN).astype(jnp.bfloat16)
    g_bdown = column_sums(d_ffn)
    d_ffn, g_down = lax.optimization_barrier((d_ffn, g_down))
    s_down = halve_core(g_down.reshape(8, -1, width))
    d_active = dot(d_ffn, mat_down, NT)
    _, gelu_back = jax.vjp(gelu_exact, gate)
    d_gate = gelu_back(d_active)[0].astype(jnp.bfloat16)
    d_gate, s_down = lax.optimization_barrier((d_gate, s_down))
    s_down = halve_first(s_down)
    g_in = dot(hidden_low, d_gate, TN).astype(jnp.bfloat16)
    g_bin = column_sums(d_gate)
    d_gate, g_in = lax.optimization_barrier((d_gate, g_in))
    s_in = halve_core(g_in.reshape(8, width // 8, -1))
    d_hidden = grad_resid_ffn + dot(d_gate, mat_in, NT)
    _, norm_attn_back = jax.vjp(layer_norm, resid_attn, gain_a, shift_a)
    grad_resid_attn, g_gain_a, g_shift_a = norm_attn_back(d_hidden)
    d_attn = grad_resid_attn.astype(jnp.bfloat16)
    g_out = dot(context, d_attn).astype(jnp.bfloat16)
    g_bout = column_sums(d_attn)
    d_context = dot(mat_out, d_attn, NT).astype(jnp.bfloat16)

    small = [g_bout, g_gain_a, g_shift_a, g_bin, g_bdown, g_gain_f, g_shift_f]
    small = jnp.concatenate([part.reshape(8, -1) for part in small], axis=1)
    own = width // 8
    g_out = jnp.concatenate(
        [g_out.reshape(8, own, width), extra_rows(small[:, :width], small[:, width:], width)],
        axis=1,
    )
    d_context, g_out, s_down, s_in = lax.optimization_barrier((d_context, g_out, s_down, s_in))
    d_mixed = lax.all_to_all(d_context, "ctx", 0, 1, tiled=True)
    s_down, s_in, s_out = halve_second(s_down), halve_first(s_in), halve_core(g_out)
    d_mixed, s_down, s_in, s_out = lax.optimization_barrier((d_mixed, s_down, s_in, s_out))

    def back_of(index):
        part = slice(index * HEAD, (index + 1) * HEAD)
        return attend_back(
            query[part], key[part], value[part], d_mixed[part], mixed[part], probs, index
        )

    s_down, s_in, s_out = sum_shares(s_down, 0), halve_second(s_in), halve_first(s_out)
    back = [back_of(0)]
    d_mixed, back, s_down, s_in, s_out = lax.optimization_barrier(
        (d_mixed, back, s_down, s_in, s_out)
    )
    s_down, s_in, s_out = gather_ctx(s_down), sum_shares(s_in, 1), halve_second(s_out)
    back.append(back_of(1))
    d_mixed, back, s_down, s_in, s_out = lax.optimization_barrier(
        (d_mixed, back, s_down, s_in, s_out)
    )
    s_in, s_out = gather_ctx(s_in), gather_ctx(s_out)
    for index in range(2, share // HEAD):
        back.append(back_of(index))
    back, s_in, s_out = lax.optimization_barrier((back, s_in, s_out))
    d_query, d_key, d_value = [
        jnp.concatenate([parts[i] for parts in back], axis=0) for i in range(3)
    ]
    d_proj = jnp.concatenate([d_query, d_key, d_value], axis=0)
    g_qkv = lax.dot_general(
        tokens_all, d_proj, (((0,), (1,)), ((), ())), preferred_element_type=jnp.float32
    ).astype(jnp.bfloat16)
    columns = 3 * share
    sums = [
        jnp.sum(part.astype(jnp.float32), axis=1).reshape(-1, own) for part in (d_query, d_value)
    ]
    first = place * (share // own)
    sums = [
        lax.dynamic_update_slice_in_dim(jnp.zeros((8, own), jnp.float32), part, first, 0)
        for part in sums
    ]
    g_qkv = jnp.concatenate(
        [g_qkv.reshape(8, own, columns), extra_rows(sums[0], sums[1], columns)], axis=1
    )
    s_qkv = halve_second(halve_first(halve_core(g_qkv)))
    spread = dot(d_proj, mat_qkv, (((0,), (1,)), ((), ()))).astype(jnp.bfloat16)
    spread = lax.all_to_all(spread.reshape(blocks, rows, width), "ctx", 0, 0, tiled=True)
    grad_tokens = grad_resid_attn + jnp.sum(spread.astype(jnp.float32), axis=0)
    all_qkv = gather_ctx(s_qkv)
    out_qkv = all_qkv[:, :own].reshape(blocks, own, 3, share).transpose(1, 2, 0, 3)
    out_qkv = out_qkv.reshape(own, 3 * width).astype(jnp.float32)
    out_query, out_value = [
        jnp.sum(all_qkv[:, own + i, :own].astype(jnp.float32), axis=0) for i in (0, 1)
    ]
    out_down = s_down.reshape(-1, width).astype(jnp.float32)
    out_in = s_in.transpose(1, 0, 2).reshape(own, -1).astype(jnp.float32)
    out_out = jnp.sum(s_out.astype(jnp.float32), axis=0)
    small = jnp.concatenate([out_out[own], out_out[own + 1]])
    ends = [edge - edges[2] for edge in edges[2:]]
    small = [small[ends[i] : ends[i + 1]] for i in range(len(ends) - 1)]
    out_out = out_out[:own]
    return (
        layer_out[None],
        grad_tokens[None],
        out_qkv,
        out_out,
        out_in,
        out_down,
        out_query,
        out_value,
        *small,
    )


def solution(mesh):
    sizes = (mesh.shape["shard"], mesh.shape["ctx"])
    chosen = local_fast if sizes == (8, 4) else local_any
    return jax.shard_map(
        chosen,
        mesh=mesh,
        in_specs=(
            P("shard", "ctx", None),
            P("shard", "ctx", None),
            P("shard", None),
            P("shard", None),
            P("shard", None),
            P("shard", None),
            P("shard", None),
            P("shard"),
            P("shard"),
            P("shard"),
            P("shard"),
            P("shard"),
            P("shard"),
            P("shard"),
            P("shard"),
            P("shard"),
        ),
        out_specs=(
            P("shard", "ctx", None),
            P("shard", "ctx", None),
            P("shard", None),
            P("shard", None),
            P("shard", None),
            P("shard", None),
            P("shard"),
            P("shard"),
            P("shard"),
            P("shard"),
            P("shard"),
            P("shard"),
            P("shard"),
            P("shard"),
            P("shard"),
        ),
        check_vma=False,
    )
```

```python
import functools

import jax
import jax.numpy as jnp
from jax import lax
from jax.experimental import pallas as pl
from jax.experimental.pallas import tpu as pltpu
from jax.sharding import PartitionSpec as P

HEADS = 12
HEAD = 64


epsilon = 1e-12
scale_attn = 0.125


def layer_norm(values, gain, shift):
    center = values - jnp.mean(values, axis=-1, keepdims=True)
    spread = jnp.mean(center * center, axis=-1, keepdims=True)
    return center * lax.rsqrt(spread + epsilon) * gain + shift


def gelu_exact(values):
    return jax.nn.gelu(values, approximate=False)


def segment_ids(counts, length):
    places = jnp.arange(length, dtype=jnp.int32)
    first_end = counts[0]
    second_end = first_end + counts[1]
    third_end = second_end + counts[2]
    return (
        (places >= first_end).astype(jnp.int32)
        + (places >= second_end).astype(jnp.int32)
        + (places >= third_end).astype(jnp.int32)
    )


def split_heads(values):
    return values.reshape(values.shape[0], HEADS, HEAD).transpose(1, 0, 2)


def join_heads(values):
    return values.transpose(1, 0, 2).reshape(values.shape[1], HEADS * HEAD)


def head_forward(query_h, key_h, value_h, match_mask):
    scores = (
        jnp.einsum("qd,kd->qk", query_h, key_h, preferred_element_type=jnp.float32) * scale_attn
    )
    scores = jnp.where(match_mask, scores, -1000000000.0)
    maximum = jnp.max(scores, axis=-1, keepdims=True)
    exp_terms = jnp.exp(scores - maximum)
    total = jnp.sum(exp_terms, axis=-1, keepdims=True)
    weights_soft = (exp_terms / total).astype(jnp.bfloat16)
    mixed = jnp.dot(weights_soft, value_h, preferred_element_type=jnp.float32)
    return (mixed, (maximum + jnp.log(total))[:, 0])


def head_backward(query_h, key_h, value_h, dctx_h, log_total, match_mask):
    scores = (
        jnp.einsum("qd,kd->qk", query_h, key_h, preferred_element_type=jnp.float32) * scale_attn
    )
    probs = jnp.where(match_mask, jnp.exp(scores - log_total[:, None]), 0.0)
    grad_probs = jnp.einsum("qd,kd->qk", dctx_h, value_h, preferred_element_type=jnp.float32)
    grad_value = jnp.einsum(
        "qk,qd->kd", probs.astype(jnp.bfloat16), dctx_h, preferred_element_type=jnp.float32
    )
    inner = jnp.sum(probs * grad_probs, axis=-1, keepdims=True)
    grad_scores = (probs * (grad_probs - inner) * scale_attn).astype(jnp.bfloat16)
    grad_query = jnp.dot(grad_scores, key_h, preferred_element_type=jnp.float32)
    grad_key = jnp.einsum("qk,qd->kd", grad_scores, query_h, preferred_element_type=jnp.float32)
    return (grad_query, grad_key, grad_value)


def column_sums(values):
    return jnp.sum(values.astype(jnp.float32), axis=0)


def local_any(
    tokens,
    cotangent,
    doc_lengths,
    w_qkv,
    w_out,
    w_in,
    w_down,
    bias_query,
    bias_value,
    bias_out,
    gain_attn,
    shift_attn,
    bias_in,
    bias_down,
    gain_ffn,
    shift_ffn,
):
    gathered = (
        lax.all_gather(w_qkv, "shard", axis=0, tiled=True),
        lax.all_gather(w_out, "shard", axis=0, tiled=True),
        lax.all_gather(w_in, "shard", axis=0, tiled=True),
        lax.all_gather(w_down, "shard", axis=0, tiled=True),
        lax.all_gather(bias_query, "shard", axis=0, tiled=True),
        lax.all_gather(bias_value, "shard", axis=0, tiled=True),
        lax.all_gather(bias_out, "shard", axis=0, tiled=True),
        lax.all_gather(gain_attn, "shard", axis=0, tiled=True),
        lax.all_gather(shift_attn, "shard", axis=0, tiled=True),
        lax.all_gather(bias_in, "shard", axis=0, tiled=True),
        lax.all_gather(bias_down, "shard", axis=0, tiled=True),
        lax.all_gather(gain_ffn, "shard", axis=0, tiled=True),
        lax.all_gather(shift_ffn, "shard", axis=0, tiled=True),
    )
    mat_qkv, mat_out, mat_in, mat_down = (gathered[0], gathered[1], gathered[2], gathered[3])
    vec_query, vec_value, vec_out, gain_a, shift_a, vec_in, vec_down, gain_f, shift_f = [
        piece.astype(jnp.float32) for piece in gathered[4:]
    ]
    rows = tokens.shape[1]
    width = tokens.shape[2]
    inputs = tokens[0]
    length = rows * lax.axis_size("ctx")
    all_ids = segment_ids(doc_lengths[0], length)
    own_ids = lax.dynamic_slice_in_dim(all_ids, lax.axis_index("ctx") * rows, rows)
    match_mask = own_ids[:, None] == all_ids[None, :]
    projected = jnp.dot(inputs, mat_qkv, preferred_element_type=jnp.float32)
    query = (projected[:, :width] + vec_query).astype(jnp.bfloat16)
    key_local = projected[:, width : 2 * width].astype(jnp.bfloat16)
    value_local = (projected[:, 2 * width :] + vec_value).astype(jnp.bfloat16)
    key_all, value_all = (
        lax.all_gather(key_local, "ctx", axis=0, tiled=True),
        lax.all_gather(value_local, "ctx", axis=0, tiled=True),
    )
    query_heads = split_heads(query)
    key_heads = split_heads(key_all)
    value_heads = split_heads(value_all)
    mixed, log_total = lax.map(
        lambda items: head_forward(items[0], items[1], items[2], match_mask),
        (query_heads, key_heads, value_heads),
    )
    context = join_heads(mixed).astype(jnp.bfloat16)
    resid_attn = inputs.astype(jnp.float32) + (
        jnp.dot(context, mat_out, preferred_element_type=jnp.float32) + vec_out
    )
    hidden = layer_norm(resid_attn, gain_a, shift_a)
    hidden_low = hidden.astype(jnp.bfloat16)
    gate = jnp.dot(hidden_low, mat_in, preferred_element_type=jnp.float32) + vec_in
    active = gelu_exact(gate).astype(jnp.bfloat16)
    resid_ffn = hidden + (jnp.dot(active, mat_down, preferred_element_type=jnp.float32) + vec_down)
    layer_out = layer_norm(resid_ffn, gain_f, shift_f).astype(jnp.bfloat16)
    regathered = (
        lax.all_gather(w_qkv, "shard", axis=0, tiled=True),
        lax.all_gather(w_out, "shard", axis=0, tiled=True),
        lax.all_gather(w_in, "shard", axis=0, tiled=True),
        lax.all_gather(w_down, "shard", axis=0, tiled=True),
    )
    mat_qkv, mat_out, mat_in, mat_down = (
        regathered[0],
        regathered[1],
        regathered[2],
        regathered[3],
    )
    upstream = cotangent[0].astype(jnp.float32)
    _, norm_ffn_back = jax.vjp(layer_norm, resid_ffn, gain_f, shift_f)
    grad_resid_ffn, g_gain_f, g_shift_f = norm_ffn_back(upstream)
    d_ffn = grad_resid_ffn.astype(jnp.bfloat16)
    g_down = jnp.einsum("tf,td->fd", active, d_ffn, preferred_element_type=jnp.float32)
    g_bdown = column_sums(d_ffn)
    d_active = jnp.einsum("td,fd->tf", d_ffn, mat_down, preferred_element_type=jnp.float32)
    _, gelu_back = jax.vjp(gelu_exact, gate)
    d_gate = gelu_back(d_active)[0].astype(jnp.bfloat16)
    g_in = jnp.einsum("td,tf->df", hidden_low, d_gate, preferred_element_type=jnp.float32)
    g_bin = column_sums(d_gate)
    d_hidden = grad_resid_ffn + jnp.einsum(
        "tf,df->td", d_gate, mat_in, preferred_element_type=jnp.float32
    )
    _, norm_attn_back = jax.vjp(layer_norm, resid_attn, gain_a, shift_a)
    grad_resid_attn, g_gain_a, g_shift_a = norm_attn_back(d_hidden)
    d_attn = grad_resid_attn.astype(jnp.bfloat16)
    g_out = jnp.einsum("tc,td->cd", context, d_attn, preferred_element_type=jnp.float32)
    g_bout = column_sums(d_attn)
    d_context = jnp.einsum("td,cd->tc", d_attn, mat_out, preferred_element_type=jnp.float32).astype(
        jnp.bfloat16
    )
    dctx_heads = split_heads(d_context)
    grad_query, grad_key, grad_value = lax.map(
        lambda items: head_backward(items[0], items[1], items[2], items[3], items[4], match_mask),
        (query_heads, key_heads, value_heads, dctx_heads, log_total),
    )
    key_terms = join_heads(grad_key)
    value_terms = join_heads(grad_value)
    key_summed, value_summed = (
        lax.psum_scatter(
            key_terms.astype(jnp.bfloat16), "ctx", scatter_dimension=0, tiled=True
        ).astype(jnp.float32),
        lax.psum_scatter(
            value_terms.astype(jnp.bfloat16), "ctx", scatter_dimension=0, tiled=True
        ).astype(jnp.float32),
    )
    d_query = join_heads(grad_query).astype(jnp.bfloat16)
    d_key = key_summed.astype(jnp.bfloat16)
    d_value = value_summed.astype(jnp.bfloat16)
    d_proj = jnp.concatenate([d_query, d_key, d_value], axis=1)
    g_qkv = jnp.einsum("td,te->de", inputs, d_proj, preferred_element_type=jnp.float32)
    g_query = column_sums(d_query)
    g_value = column_sums(d_value)
    grad_tokens = grad_resid_attn + jnp.einsum(
        "te,de->td", d_proj, mat_qkv, preferred_element_type=jnp.float32
    )
    group_parts = (
        lax.psum_scatter(
            g_qkv.astype(jnp.bfloat16), "shard", scatter_dimension=0, tiled=True
        ).astype(jnp.float32),
        lax.psum_scatter(
            g_out.astype(jnp.bfloat16), "shard", scatter_dimension=0, tiled=True
        ).astype(jnp.float32),
        lax.psum_scatter(
            g_in.astype(jnp.bfloat16), "shard", scatter_dimension=0, tiled=True
        ).astype(jnp.float32),
        lax.psum_scatter(
            g_down.astype(jnp.bfloat16), "shard", scatter_dimension=0, tiled=True
        ).astype(jnp.float32),
        lax.psum_scatter(
            g_query.astype(jnp.bfloat16), "shard", scatter_dimension=0, tiled=True
        ).astype(jnp.float32),
        lax.psum_scatter(
            g_value.astype(jnp.bfloat16), "shard", scatter_dimension=0, tiled=True
        ).astype(jnp.float32),
        lax.psum_scatter(
            g_bout.astype(jnp.bfloat16), "shard", scatter_dimension=0, tiled=True
        ).astype(jnp.float32),
        lax.psum_scatter(
            g_gain_a.astype(jnp.bfloat16), "shard", scatter_dimension=0, tiled=True
        ).astype(jnp.float32),
        lax.psum_scatter(
            g_shift_a.astype(jnp.bfloat16), "shard", scatter_dimension=0, tiled=True
        ).astype(jnp.float32),
        lax.psum_scatter(
            g_bin.astype(jnp.bfloat16), "shard", scatter_dimension=0, tiled=True
        ).astype(jnp.float32),
        lax.psum_scatter(
            g_bdown.astype(jnp.bfloat16), "shard", scatter_dimension=0, tiled=True
        ).astype(jnp.float32),
        lax.psum_scatter(
            g_gain_f.astype(jnp.bfloat16), "shard", scatter_dimension=0, tiled=True
        ).astype(jnp.float32),
        lax.psum_scatter(
            g_shift_f.astype(jnp.bfloat16), "shard", scatter_dimension=0, tiled=True
        ).astype(jnp.float32),
    )
    (
        p_qkv,
        p_out,
        p_in,
        p_down,
        p_query,
        p_value,
        p_bout,
        p_gain_a,
        p_shift_a,
        p_bin,
        p_bdown,
        p_gain_f,
        p_shift_f,
    ) = group_parts
    summed = (
        lax.psum(p_qkv.astype(jnp.bfloat16), "ctx").astype(jnp.float32),
        lax.psum(p_out.astype(jnp.bfloat16), "ctx").astype(jnp.float32),
        lax.psum(p_in.astype(jnp.bfloat16), "ctx").astype(jnp.float32),
        lax.psum(p_down.astype(jnp.bfloat16), "ctx").astype(jnp.float32),
        lax.psum(p_query.astype(jnp.bfloat16), "ctx").astype(jnp.float32),
        lax.psum(p_value.astype(jnp.bfloat16), "ctx").astype(jnp.float32),
        lax.psum(p_bout.astype(jnp.bfloat16), "ctx").astype(jnp.float32),
        lax.psum(p_gain_a.astype(jnp.bfloat16), "ctx").astype(jnp.float32),
        lax.psum(p_shift_a.astype(jnp.bfloat16), "ctx").astype(jnp.float32),
        lax.psum(p_bin.astype(jnp.bfloat16), "ctx").astype(jnp.float32),
        lax.psum(p_bdown.astype(jnp.bfloat16), "ctx").astype(jnp.float32),
        lax.psum(p_gain_f.astype(jnp.bfloat16), "ctx").astype(jnp.float32),
        lax.psum(p_shift_f.astype(jnp.bfloat16), "ctx").astype(jnp.float32),
    )
    return (
        layer_out[None],
        grad_tokens[None],
        summed[0],
        summed[1],
        summed[2],
        summed[3],
        summed[4],
        summed[5],
        summed[6],
        summed[7],
        summed[8],
        summed[9],
        summed[10],
        summed[11],
        summed[12],
    )


QUERY_BLOCK = 256
VMEM_BYTES = 56 * 1024 * 1024
TN = (((0,), (0,)), ((), ()))
NT = (((1,), (1,)), ((), ()))


def dot(a, b, dims=(((1,), (0,)), ((), ()))):
    return lax.dot_general(a, b, dims, preferred_element_type=jnp.float32)


def attend_kernel(ids_row, ids_col, q_ref, k_ref, v_ref, ctx_ref, p_ref):
    scores = dot(k_ref[...], q_ref[...] * jnp.bfloat16(0.125), TN)
    scores = jnp.where(ids_col[...] == ids_row[...], scores, -1000000000.0)
    maximum = jnp.max(scores, axis=0, keepdims=True)
    terms = jnp.exp(scores - maximum)
    total = jnp.sum(terms, axis=0, keepdims=True)
    probs = (terms * (1.0 / total)).astype(jnp.bfloat16)
    p_ref[0] = probs
    ctx_ref[...] = dot(v_ref[...], probs).astype(jnp.bfloat16)


def attend(ids, q, k, v):
    width, length = q.shape
    heads = width // HEAD
    block = QUERY_BLOCK
    row = pl.BlockSpec((HEAD, length), lambda h, b: (h, 0))
    part = pl.BlockSpec((HEAD, block), lambda h, b: (h, b))
    return pl.pallas_call(
        attend_kernel,
        grid=(heads, length // block),
        in_specs=[
            pl.BlockSpec((1, block), lambda h, b: (0, b)),
            pl.BlockSpec((length, 1), lambda h, b: (0, 0)),
            part,
            row,
            row,
        ],
        out_specs=[part, pl.BlockSpec((1, length, block), lambda h, b: (h, 0, b))],
        out_shape=[
            jax.ShapeDtypeStruct((width, length), jnp.bfloat16),
            jax.ShapeDtypeStruct((heads, length, length), jnp.bfloat16),
        ],
        compiler_params=pltpu.CompilerParams(vmem_limit_bytes=VMEM_BYTES),
        cost_estimate=pl.CostEstimate(
            flops=heads * length * length * 256 * 4,
            bytes_accessed=heads * length * length * 4,
            transcendentals=heads * length * length,
        ),
        name="attend",
    )(ids[None, :], ids[:, None], q, k, v)


def attend_back_kernel(
    q_ref, k_ref, v_ref, d_ref, ctx_ref, p_ref, dq_ref, dk_ref, dv_ref, dk_sum, dv_sum
):
    step = pl.program_id(1)

    @pl.when(step == 0)
    def _():
        dk_sum[...] = jnp.zeros_like(dk_sum)
        dv_sum[...] = jnp.zeros_like(dv_sum)

    probs = p_ref[0]
    d_ctx = d_ref[...]
    inner = jnp.sum(
        d_ctx.astype(jnp.float32) * ctx_ref[...].astype(jnp.float32), axis=0, keepdims=True
    )
    d_probs = dot(v_ref[...], d_ctx, TN)
    d_scores = (probs.astype(jnp.float32) * (d_probs - inner)).astype(jnp.bfloat16)
    dq_ref[...] = (dot(k_ref[...], d_scores) * 0.125).astype(jnp.bfloat16)
    dk_sum[...] += dot(d_scores, q_ref[...], NT)
    dv_sum[...] += dot(probs, d_ctx, NT)

    @pl.when(step == pl.num_programs(1) - 1)
    def _():
        dk_ref[...] = (dk_sum[...].T * 0.125).astype(jnp.bfloat16)
        dv_ref[...] = dv_sum[...].T.astype(jnp.bfloat16)


def attend_back(q, k, v, d_ctx, ctx, probs):
    width, length = q.shape
    heads = width // HEAD
    block = QUERY_BLOCK
    row = pl.BlockSpec((HEAD, length), lambda h, b: (h, 0))
    part = pl.BlockSpec((HEAD, block), lambda h, b: (h, b))
    shape = jax.ShapeDtypeStruct((width, length), jnp.bfloat16)
    return pl.pallas_call(
        attend_back_kernel,
        grid=(heads, length // block),
        in_specs=[
            part,
            row,
            row,
            part,
            part,
            pl.BlockSpec((1, length, block), lambda h, b: (h, 0, b)),
        ],
        out_specs=[part, row, row],
        out_shape=[shape, shape, shape],
        scratch_shapes=[pltpu.VMEM((length, HEAD), jnp.float32)] * 2,
        compiler_params=pltpu.CompilerParams(vmem_limit_bytes=VMEM_BYTES),
        cost_estimate=pl.CostEstimate(
            flops=heads * length * length * 256 * 10,
            bytes_accessed=heads * length * length * 4,
            transcendentals=0,
        ),
        name="attend_back",
    )(q, k, v, d_ctx, ctx, probs)


def swap(values, bit):
    return lax.ppermute(values, "shard", [(i, i ^ bit) for i in range(8)])


def place_kernel(*refs):
    *pieces, whole, sems = refs
    me = lax.axis_index("shard")
    rows = pieces[0].shape[0]
    half = rows // 2
    copies = []
    for core in (0, 1):
        own, over_x, over_y, top, bottom = pieces[core * 5 : core * 5 + 5]
        for piece, bits, shift in (
            (own, 0, 0),
            (over_x, 2, 0),
            (over_y, 4, 0),
            (top, 6, 0),
            (bottom, 6, half),
        ):
            owner = flip(me, bits + core)
            start = pl.multiple_of(owner * rows + shift, 16)
            copies.append(
                pltpu.make_async_copy(
                    piece, whole.at[pl.ds(start, piece.shape[0])], sems.at[len(copies)]
                )
            )
    for copy in copies:
        copy.start()
    for copy in copies:
        copy.wait()


def flip(index, bits):
    result = index
    for bit in (1, 2, 4):
        if bits & bit:
            held = lax.rem(index // bit, 2)
            result = result + bit - 2 * bit * held
    return result


def gather_shard(piece):
    rows, columns = piece.shape
    half = rows // 2
    over_x = swap(piece, 2)
    over_y = swap(piece, 4)
    top = swap(over_x[:half], 4)
    bottom = swap(over_y[half:], 2)
    near = [piece, over_x, over_y, top, bottom]
    far = [swap(part, 1) for part in near]
    return pl.pallas_call(
        place_kernel,
        in_specs=[pl.BlockSpec(memory_space=pl.ANY)] * 10,
        out_specs=pl.BlockSpec(memory_space=pltpu.VMEM),
        compiler_params=pltpu.CompilerParams(vmem_limit_bytes=VMEM_BYTES),
        out_shape=jax.ShapeDtypeStruct((8 * rows, columns), piece.dtype),
        scratch_shapes=[pltpu.SemaphoreType.DMA((10,))],
        cost_estimate=pl.CostEstimate(
            flops=0, bytes_accessed=32 * rows * columns, transcendentals=0
        ),
        name="place_rows",
    )(*near, *far)


def add_low(a, b):
    return (a.astype(jnp.float32) + b.astype(jnp.float32)).astype(jnp.bfloat16)


def pick(values, index, axis):
    return lax.dynamic_index_in_dim(values, index, axis, keepdims=False)


def scatter_shard(whole):
    me = lax.axis_index("shard")
    core, x, y = me % 2, (me // 2) % 2, me // 4
    _, rows, columns = whole.shape
    half = rows // 32 * 16
    parts = whole.reshape(4, 2, rows, columns)
    mine = add_low(pick(parts, core, 1), swap(pick(parts, 1 - core, 1), 1))
    mine = mine.reshape(2, 2, rows, columns)
    left, right = mine[:, :, :half], mine[:, :, half:]
    left = add_low(pick(left, x, 1), swap(pick(left, 1 - x, 1), 2))
    right = add_low(pick(right, y, 0), swap(pick(right, 1 - y, 0), 4))
    left = add_low(pick(left, y, 0), swap(pick(left, 1 - y, 0), 4))
    right = add_low(pick(right, x, 0), swap(pick(right, 1 - x, 0), 2))
    return jnp.concatenate([left, right], axis=0)


def share_vector(vector):
    rows = jnp.zeros((8, vector.shape[0]), vector.dtype)
    rows = lax.dynamic_update_slice_in_dim(rows, vector[None], lax.axis_index("shard"), 0)
    for bit in (1, 2, 4):
        rows = rows + swap(rows, bit)
    return rows


def gather_ctx(piece):
    copies = jnp.broadcast_to(piece[None], (lax.axis_size("ctx"), *piece.shape))
    return lax.all_to_all(copies, "ctx", 0, 0, tiled=True)


def extra_rows(first, second, columns):
    rows = [jnp.pad(part, ((0, 0), (0, columns - part.shape[1]))) for part in (first, second)]
    return jnp.pad(jnp.stack(rows, axis=1), ((0, 0), (0, 14), (0, 0))).astype(jnp.bfloat16)


def local_fast(
    tokens,
    cotangent,
    doc_lengths,
    w_qkv,
    w_out,
    w_in,
    w_down,
    bias_query,
    bias_value,
    bias_out,
    gain_attn,
    shift_attn,
    bias_in,
    bias_down,
    gain_ffn,
    shift_ffn,
):
    blocks = lax.axis_size("ctx")
    place = lax.axis_index("ctx")
    inputs = tokens[0]
    rows, width = inputs.shape
    length = rows * blocks
    share = width // blocks
    vectors = [
        bias_query,
        bias_value,
        bias_out,
        gain_attn,
        shift_attn,
        bias_in,
        bias_down,
        gain_ffn,
        shift_ffn,
    ]
    sizes = [vector.shape[0] for vector in vectors]

    tokens_all = gather_ctx(inputs).reshape(length, width)
    qkv_part = lax.dynamic_index_in_dim(
        w_qkv.reshape(w_qkv.shape[0], 3, blocks, share), place, 2, keepdims=False
    ).reshape(w_qkv.shape[0], 3 * share)
    mat_qkv = gather_shard(qkv_part)
    packed = share_vector(jnp.concatenate(vectors))
    mat_out = gather_shard(w_out)
    mat_in = gather_shard(w_in)
    mat_down = gather_shard(w_down)
    edges = [sum(sizes[:i]) for i in range(len(sizes) + 1)]
    vec_query, vec_value, vec_out, gain_a, shift_a, vec_in, vec_down, gain_f, shift_f = [
        packed[:, edges[i] : edges[i + 1]].reshape(-1).astype(jnp.float32)
        for i in range(len(sizes))
    ]

    ids = segment_ids(doc_lengths[0], length)
    bias_q = lax.dynamic_slice_in_dim(vec_query, place * share, share)
    bias_v = lax.dynamic_slice_in_dim(vec_value, place * share, share)
    proj = lax.dot_general(
        mat_qkv, tokens_all, (((0,), (1,)), ((), ())), preferred_element_type=jnp.float32
    )
    query = (proj[:share] + bias_q[:, None]).astype(jnp.bfloat16)
    key = proj[share : 2 * share].astype(jnp.bfloat16)
    value = (proj[2 * share :] + bias_v[:, None]).astype(jnp.bfloat16)
    mixed, probs = attend(ids, query, key, value)
    context = lax.all_to_all(mixed, "ctx", 1, 0, tiled=True)

    resid_attn = inputs.astype(jnp.float32) + (dot(context, mat_out, TN) + vec_out)
    hidden = layer_norm(resid_attn, gain_a, shift_a)
    hidden_low = hidden.astype(jnp.bfloat16)
    gate = dot(hidden_low, mat_in) + vec_in
    active = gelu_exact(gate).astype(jnp.bfloat16)
    resid_ffn = hidden + (dot(active, mat_down) + vec_down)
    layer_out = layer_norm(resid_ffn, gain_f, shift_f).astype(jnp.bfloat16)

    upstream = cotangent[0].astype(jnp.float32)
    _, norm_ffn_back = jax.vjp(layer_norm, resid_ffn, gain_f, shift_f)
    grad_resid_ffn, g_gain_f, g_shift_f = norm_ffn_back(upstream)
    d_ffn = grad_resid_ffn.astype(jnp.bfloat16)
    g_down = dot(active, d_ffn, TN).astype(jnp.bfloat16)
    g_bdown = column_sums(d_ffn)
    d_ffn, g_down = lax.optimization_barrier((d_ffn, g_down))
    s_down = scatter_shard(g_down.reshape(8, -1, width))
    d_active = dot(d_ffn, mat_down, NT)
    _, gelu_back = jax.vjp(gelu_exact, gate)
    d_gate = gelu_back(d_active)[0].astype(jnp.bfloat16)
    g_in = dot(hidden_low, d_gate, TN).astype(jnp.bfloat16)
    g_bin = column_sums(d_gate)
    d_gate, g_in = lax.optimization_barrier((d_gate, g_in))
    s_in = scatter_shard(g_in.reshape(8, width // 8, -1))
    d_hidden = grad_resid_ffn + dot(d_gate, mat_in, NT)
    _, norm_attn_back = jax.vjp(layer_norm, resid_attn, gain_a, shift_a)
    grad_resid_attn, g_gain_a, g_shift_a = norm_attn_back(d_hidden)
    d_attn = grad_resid_attn.astype(jnp.bfloat16)
    g_out = dot(context, d_attn).astype(jnp.bfloat16)
    g_bout = column_sums(d_attn)
    d_context = dot(mat_out, d_attn, NT).astype(jnp.bfloat16)

    d_mixed = lax.all_to_all(d_context, "ctx", 0, 1, tiled=True)
    small = [g_bout, g_gain_a, g_shift_a, g_bin, g_bdown, g_gain_f, g_shift_f]
    small = jnp.concatenate([part.reshape(8, -1) for part in small], axis=1)
    own = width // 8
    g_out = jnp.concatenate(
        [g_out.reshape(8, own, width), extra_rows(small[:, :width], small[:, width:], width)],
        axis=1,
    )
    s_out = scatter_shard(g_out)
    d_query, d_key, d_value = attend_back(query, key, value, d_mixed, mixed, probs)
    d_proj = jnp.concatenate([d_query, d_key, d_value], axis=0)
    spread = dot(d_proj, mat_qkv, (((0,), (1,)), ((), ()))).astype(jnp.bfloat16)
    spread, d_proj = lax.optimization_barrier((spread, d_proj))
    spread = lax.all_to_all(spread.reshape(blocks, rows, width), "ctx", 0, 0, tiled=True)
    g_qkv = lax.dot_general(
        tokens_all, d_proj, (((0,), (1,)), ((), ())), preferred_element_type=jnp.float32
    ).astype(jnp.bfloat16)
    columns = 3 * share
    sums = [
        jnp.sum(part.astype(jnp.float32), axis=1).reshape(-1, own) for part in (d_query, d_value)
    ]
    first = place * (share // own)
    sums = [
        lax.dynamic_update_slice_in_dim(jnp.zeros((8, own), jnp.float32), part, first, 0)
        for part in sums
    ]
    g_qkv = jnp.concatenate(
        [g_qkv.reshape(8, own, columns), extra_rows(sums[0], sums[1], columns)], axis=1
    )
    s_qkv = scatter_shard(g_qkv)
    spread, s_qkv = lax.optimization_barrier((spread, s_qkv))
    grad_tokens = grad_resid_attn + jnp.sum(spread.astype(jnp.float32), axis=0)
    all_qkv = gather_ctx(s_qkv)
    out_qkv = all_qkv[:, :own].reshape(blocks, own, 3, share).transpose(1, 2, 0, 3)
    out_qkv = out_qkv.reshape(own, 3 * width).astype(jnp.float32)
    out_query, out_value = [
        jnp.sum(all_qkv[:, own + i, :own].astype(jnp.float32), axis=0) for i in (0, 1)
    ]
    out_down, out_in, out_out = [
        part.astype(jnp.float32) for part in lax.psum((s_down, s_in, s_out), "ctx")
    ]
    small = jnp.concatenate([out_out[own], out_out[own + 1]])
    ends = [edge - edges[2] for edge in edges[2:]]
    small = [small[ends[i] : ends[i + 1]] for i in range(len(ends) - 1)]
    out_out = out_out[:own]
    return (
        layer_out[None],
        grad_tokens[None],
        out_qkv,
        out_out,
        out_in,
        out_down,
        out_query,
        out_value,
        *small,
    )


def solution(mesh):
    sizes = (mesh.shape["shard"], mesh.shape["ctx"])
    chosen = local_fast if sizes == (8, 4) else local_any
    return jax.shard_map(
        chosen,
        mesh=mesh,
        in_specs=(
            P("shard", "ctx", None),
            P("shard", "ctx", None),
            P("shard", None),
            P("shard", None),
            P("shard", None),
            P("shard", None),
            P("shard", None),
            P("shard"),
            P("shard"),
            P("shard"),
            P("shard"),
            P("shard"),
            P("shard"),
            P("shard"),
            P("shard"),
            P("shard"),
        ),
        out_specs=(
            P("shard", "ctx", None),
            P("shard", "ctx", None),
            P("shard", None),
            P("shard", None),
            P("shard", None),
            P("shard", None),
            P("shard"),
            P("shard"),
            P("shard"),
            P("shard"),
            P("shard"),
            P("shard"),
            P("shard"),
            P("shard"),
            P("shard"),
        ),
        check_vma=False,
    )
```
